512 devices in a mesh: lev: 8 (over x, core), tile: 64 (over z, y).
Axes of the slice: x: 4, y: 4, z: 16, core: 2. Of those that a mesh axis runs over, the one named last changes fastest.
Arguments:
- lam_in: float32 [4, 48, 1024, 1024], P(None, 'lev', 'tile'), may hold values from -6 to 6
- courant_x: float32 [48, 1024, 1024], P('lev', 'tile'), may hold values from -0.15 to 0.15
- courant_y: float32 [48, 1024, 1024], P('lev', 'tile'), may hold values from -0.15 to 0.15
- kz_face: float32 [48, 1024, 1024], P('lev', 'tile'), may hold values from 0.02 to 0.15
- loss_rate: float32 [4, 48], P(None, 'lev'), may hold values from 0.05 to 1
- profile: float32 [4, 48], P(None, 'lev'), may hold values from 0.1 to 1
- kernel: float32 [48], P('lev'), may hold values from 0.3 to 1.5
- obs_values: bfloat16 [524288, 128], P(('lev', 'tile')), may hold values from -0.75 to 0.75
- obs_tile: int32 [524288, 1], P(('lev', 'tile')), may hold values from 0 to 63, as said below
- obs_block: int32 [524288], P(('lev', 'tile')), may hold values from 0 to 127
Outputs:
- lam_out: float32 [4, 48, 1024, 1024], P(None, 'lev', 'tile')
- emis_grad: float32 [4, 1024, 1024], P(None, 'tile', 'lev')
The draws below stay inside these ranges and needn't reach their ends.
Inputs may be any that keep to these rules, and one draw needn't show every extreme that they name: `obs_tile`: of the 1024 rows of one device (aligned blocks of 1024 rows), at most 64 name any one tile, and one tile is named exactly 64 times in every block.
All inputs are finite; a program needn't handle non-finite values.
Results may differ from the reference program's by a relative error of at most 0.0015.
Values may be sent and summed in bfloat16 or wider, within the bound.
No kernel may reach another device: no remote copies, remote signals or barrier semaphores. Data moves between devices by JAX's collectives and lax.ppermute only.
A program may use at most 64 MiB of HBM per device.

```python
import math
import jax
import jax.numpy as jnp
from jax import lax

NTR = 4
PIX = 128
STEPS = 2
NY = 1024
OBS_DEV = 1024
NX = 1024
NLEV = 48
TILES = 64
NB = 128
CAP = 64
OBS = 524288


def draw_obs_tile(key, part):
    key = jax.random.fold_in(key, 11)
    band_key, hot_key, row_key = jax.random.split(key, 3)
    slot_count = TILES * CAP
    band_width = max(TILES // 4, 1)
    anchor = jax.random.randint(band_key, (), 0, TILES)
    offset = jax.random.randint(hot_key, (), 0, band_width)
    tile_of_slot = jnp.arange(slot_count, dtype=jnp.int32) // CAP
    tropical = (tile_of_slot - anchor) % TILES < band_width
    hottest = (anchor + offset) % TILES
    weights = jnp.where(tropical, 3, 1).astype(jnp.int32)
    priority = jnp.where(tile_of_slot == hottest, 16384, 0).astype(jnp.int32)
    device_count = OBS // OBS_DEV

    def draw_device(device_key):
        random_part = jax.random.randint(device_key, (slot_count,), 0, 4096)
        ranking = (random_part * weights + priority) * 8192 + jnp.arange(slot_count, dtype=jnp.int32)
        values_unused, picked = lax.top_k(ranking, OBS_DEV)
        return tile_of_slot[picked]
    device_keys = jax.random.split(row_key, device_count)
    return jax.vmap(draw_device)(device_keys).reshape(OBS, 1).astype(jnp.int32)


def plant(values, stream_key, least, largest):
    longest = values.shape.index(max(values.shape))
    spots = []
    for shift in (0, 1):
        where = [jax.random.randint(jax.random.fold_in(stream_key, axis), (), 0, length) for axis, length in enumerate(values.shape)]
        where[longest] = (where[longest] + shift) % values.shape[longest]
        spots.append(tuple(where))
    return values.at[spots[0]].set(least).at[spots[1]].set(largest)


def shard_levels(key, extent, cuts, low, largest):
    loudness, own = 1.0, jax.random.fold_in(key, 6)
    for dim, shards_of in cuts:
        steps = jnp.exp(jax.random.uniform(jax.random.fold_in(own, dim), (shards_of,), jnp.float32, low / len(cuts), largest / len(cuts)))
        loudness = loudness * jnp.repeat(steps, extent[dim] // shards_of).reshape([-1 if axis == dim else 1 for axis in range(len(extent))])
    return loudness


def bell_draw(stream_key, extent, deviation, most, pieces=(), kind=jnp.bfloat16):
    values = jax.random.normal(stream_key, extent, jnp.float32) * deviation
    if len(pieces) > 0:
        values = shard_levels(stream_key, extent, pieces, -0.22, 0.18) * values
    return jnp.clip(values, min=-most, max=most).astype(kind)


def setup_inputs(seed: int = 0) -> dict:
    key_list = jax.random.split(jax.random.key(seed), 11)
    lam_in = bell_draw(key_list[0], (NTR, NLEV, NX, NY), 1.0, 6.0, ((1, 8), (2, 64)), jnp.float32)
    courant_x = jnp.clip(jax.random.uniform(key_list[1], (NLEV, NX, NY), jnp.float32, -0.15, 0.15) * shard_levels(key_list[1], (NLEV, NX, NY), ((0, 8), (1, 64)), -0.4, 0.0), -0.15, 0.15)
    courant_y = jnp.clip(jax.random.uniform(key_list[2], (NLEV, NX, NY), jnp.float32, -0.15, 0.15) * shard_levels(key_list[2], (NLEV, NX, NY), ((0, 8), (1, 64)), -0.4, 0.0), -0.15, 0.15)
    kz_face = jnp.clip(0.02 + 0.13000001 * jax.random.uniform(key_list[3], (NLEV, NX, NY), jnp.float32) ** shard_levels(key_list[3], (NLEV, NX, NY), ((0, 8), (1, 64)), -0.2, 0.2), 0.02, 0.15)
    loss_rate = jnp.clip(jnp.exp(math.log(1.0) - 2.9957323 * jax.random.uniform(key_list[4], (NTR, NLEV), jnp.float32) ** shard_levels(key_list[4], (NTR, NLEV), ((1, 8),), -0.2, 0.2)), 0.05, 1.0)
    profile = jnp.clip(jnp.exp(math.log(1.0) - 2.3025851 * jax.random.uniform(key_list[5], (NTR, NLEV), jnp.float32) ** shard_levels(key_list[5], (NTR, NLEV), ((1, 8),), -0.2, 0.2)), 0.1, 1.0)
    kernel = jnp.clip(jnp.exp(math.log(1.5) - 1.60943787 * jax.random.uniform(key_list[6], (NLEV,), jnp.float32) ** shard_levels(key_list[6], (NLEV,), ((0, 8),), -0.2, 0.2)), 0.3, 1.5)
    obs_values = bell_draw(key_list[7], (OBS, PIX), 0.125, 0.75, ((0, 512),))
    obs_tile = draw_obs_tile(jax.random.fold_in(key_list[10], 71), 0)
    obs_block = plant(jax.random.randint(key_list[9], (OBS,), 0, NB), jax.random.fold_in(key_list[9], 1), 0, NB - 1).astype(jnp.int32)
    return dict(lam_in=lam_in, courant_x=courant_x, courant_y=courant_y, kz_face=kz_face, loss_rate=loss_rate, profile=profile, kernel=kernel, obs_values=obs_values, obs_tile=obs_tile, obs_block=obs_block)


def adjoint_step(adjoint, decay_factor, kz_masked, courant_east, courant_north):
    scaled = decay_factor * adjoint
    level_pad = jnp.pad(scaled, ((0, 0), (1, 1), (0, 0), (0, 0)))
    kz_below = jnp.pad(kz_masked[:-1], ((1, 0), (0, 0), (0, 0)))
    mixed = scaled + kz_masked * (level_pad[:, 2:] - scaled) - kz_below * (scaled - level_pad[:, :-2])
    row_pad = jnp.pad(mixed, ((0, 0), (0, 0), (1, 1), (0, 0)))
    col_pad = jnp.pad(mixed, ((0, 0), (0, 0), (0, 0), (1, 1)))
    courant_west = jnp.pad(courant_east[:, :-1], ((0, 0), (1, 0), (0, 0)))
    courant_south = jnp.pad(courant_north[:, :, :-1], ((0, 0), (0, 0), (1, 0)))
    result = mixed + jnp.maximum(courant_east, 0.0) * (row_pad[:, :, 2:] - mixed)
    result = result + jnp.minimum(courant_west, 0.0) * (mixed - row_pad[:, :, :-2])
    result = result + jnp.maximum(courant_north, 0.0) * (col_pad[:, :, :, 2:] - mixed)
    result = result + jnp.minimum(courant_south, 0.0) * (mixed - col_pad[:, :, :, :-2])
    return result


def reference(lam_in, courant_x, courant_y, kz_face, loss_rate, profile, kernel, obs_values, obs_tile, obs_block):
    flat_index = (obs_tile[:, 0] * NB + obs_block).astype(jnp.int32)
    pixel_map = jax.ops.segment_sum(obs_values.astype(jnp.float32), flat_index, num_segments=TILES * NB)
    field_map = pixel_map.reshape(NX, NY)
    courant_east = jnp.where((jnp.arange(NX) == NX - 1)[None, :, None], 0.0, courant_x)
    courant_north = jnp.where((jnp.arange(NY) == NY - 1)[None, None, :], 0.0, courant_y)
    kz_masked = jnp.where((jnp.arange(NLEV) == NLEV - 1)[:, None, None], 0.0, kz_face)
    adjoint = lam_in + kernel[None, :, None, None] * field_map[None, None]
    decay_factor = jnp.exp(-loss_rate)[:, :, None, None]
    weights = profile[:, :, None, None]
    gradient = jnp.zeros((NTR, NX, NY), jnp.float32)
    for step_index in range(STEPS):
        gradient = gradient + jnp.sum(weights * adjoint, axis=1)
        adjoint = adjoint_step(adjoint, decay_factor, kz_masked, courant_east, courant_north)
    return adjoint, gradient
```

```python
import functools

import jax
import jax.numpy as jnp
import numpy as np
from jax import lax
from jax.experimental import pallas as pl
from jax.experimental.pallas import tpu as pltpu
from jax.sharding import Mesh
from jax.sharding import PartitionSpec as P

SPLIT = (4, 2, 16, 4)
SHIFTS = ((0, 8), (4, 12), (1, 9), (7, 15), (2, 10), (6, 14), (3, 11), (5, 13))
CAP = 64
LEV = ("x", "core")
TILE = ("z", "y")
ROWS = 24
VMEM = 48 * 1024 * 1024


def chain(axes, count, steps):
    first, last = max(0, -steps), min(count, count - steps)
    return functools.partial(
        lax.ppermute, axis_name=axes, perm=[(i, i + steps) for i in range(first, last)]
    )


def pack_kernel(tile_ref, block_ref, base_ref, obs_ref, out_ref):
    tiles = base_ref.shape[0]
    members, depth, _ = out_ref.shape
    count = obs_ref.shape[0]
    pair = 2 * CAP
    tile = tile_ref[...]
    block = block_ref[...]
    hot = lax.broadcasted_iota(jnp.int32, (tiles, count), 0) == tile
    before = lax.broadcasted_iota(jnp.int32, (count, count), 0) < lax.broadcasted_iota(
        jnp.int32, (count, count), 1
    )
    rank = jnp.dot(
        hot.astype(jnp.bfloat16), before.astype(jnp.bfloat16), preferred_element_type=jnp.float32
    )
    place = jnp.sum(jnp.where(hot, rank + base_ref[...], 0.0), axis=0, keepdims=True)
    place = place.astype(jnp.int32)
    member = place // pair
    slot = place - member * pair
    code = (block + 1 + jnp.where(slot >= CAP, 128, 0)).astype(jnp.float32)
    owns = lax.broadcasted_iota(jnp.int32, (members, count), 0) == member
    at = lax.broadcasted_iota(jnp.int32, (pair, count), 0) == slot
    codes = lax.dot_general(
        owns.astype(jnp.bfloat16),
        jnp.where(at, code, 0.0).astype(jnp.bfloat16),
        (((1,), (1,)), ((), ())),
        preferred_element_type=jnp.float32,
    ).astype(jnp.bfloat16)
    out_ref[:, pair:, :] = jnp.broadcast_to(codes[:, None, :], (members, depth - pair, 128))
    group = min(4, members)

    def body(g, _):
        rows = lax.broadcasted_iota(jnp.int32, (group * pair, count), 0)
        pick = rows == place - g * (group * pair)
        got = jnp.dot(
            pick.astype(jnp.bfloat16), obs_ref[...], preferred_element_type=jnp.float32
        ).astype(jnp.bfloat16)
        out_ref[pl.ds(g * group, group), :pair, :] = got.reshape(group, pair, 128)
        return 0

    lax.fori_loop(0, members // group, body, 0)


def sum_kernel(got_ref, out_ref):
    sources = got_ref.shape[0]
    pair = 2 * CAP
    total = jnp.zeros((256, 128), jnp.float32)
    for s in range(0, sources, 2):
        code = jnp.concatenate(
            [got_ref[s + i, pair : pair + 16, :].astype(jnp.float32)[:1] for i in range(2)], axis=1
        )
        pick = lax.broadcasted_iota(jnp.int32, (256, 2 * pair), 0) + 1 == code.astype(jnp.int32)
        rows = jnp.concatenate([got_ref[s + i, :pair, :] for i in range(2)], axis=0)
        total += jnp.dot(pick.astype(jnp.bfloat16), rows, preferred_element_type=jnp.float32)
    out_ref[...] = total.reshape(2, 128, 128)


def roll(x, shift, axis):
    return pltpu.roll(x, shift % x.shape[axis], axis)


def step_kernel(
    decay_ref,
    gain_ref,
    profile_ref,
    lam_ref,
    kz_ref,
    cx_ref,
    cy_ref,
    low_ref,
    high_ref,
    rim_ref,
    map_ref,
    out_ref,
    surface_ref,
    kzs,
    cxs,
    cys,
    blocks,
    field,
    scaled,
    later,
    mixed,
    moved,
):
    f32 = jnp.float32
    cols = lam_ref.shape[3]
    groups, parts = cols // 128, map_ref.shape[0]

    total = map_ref[0]
    for k in range(1, parts):
        total = total + map_ref[k]
    blocks[0:144, :] = total[0:144]
    blocks[144:176, :] = jnp.zeros((32, 128), f32)
    blocks[176:192, :] = total[144:160]
    for q in range(groups):
        field[:, q * 128 : (q + 1) * 128] = blocks[pl.ds(q, ROWS, stride=groups), :]

    def put(ref, at, body, plane):
        ref[at, 0:16, :] = body.astype(f32)
        ref[at, 16:24, :] = rim_ref[plane].astype(f32)

    for l in range(9):
        body = low_ref[8 + l] if l < 2 else (kz_ref[l - 2] if l < 8 else high_ref[8])
        put(kzs, l, body, 40 + l)
    for l in range(8):
        put(cxs, l, low_ref[10] if l < 1 else (cx_ref[l - 1] if l < 7 else high_ref[9]), 49 + l)
        put(cys, l, low_ref[11] if l < 1 else (cy_ref[l - 1] if l < 7 else high_ref[10]), 57 + l)

    def mix(ref, at, kz_at):
        here = ref[at]
        return here + kzs[kz_at] * (ref[at + 1] - here) - kzs[kz_at - 1] * (here - ref[at - 1])

    def advect(m, at):
        cx = cxs[at]
        gx = roll(m, -1, 0) - m
        value = m + jnp.maximum(cx, 0.0) * gx + roll(jnp.minimum(cx, 0.0) * gx, 1, 0)
        cy = cys[at]
        gy = roll(m, -1, 1) - m
        return value + jnp.maximum(cy, 0.0) * gy + roll(jnp.minimum(cy, 0.0) * gy, 1, 1)

    def tracer(c, _):
        total = jnp.zeros((16, cols), f32)
        for l in range(10):
            if l < 2:
                body = low_ref[c * 2 + l].astype(f32)
            elif l < 8:
                body = lam_ref[c, l - 2]
            else:
                body = high_ref[c * 2 + l - 8].astype(f32)
            own = body + gain_ref[l] * field[0:16, :]
            if 2 <= l < 8:
                total = total + profile_ref[c * 6 + l - 2] * own
            rim = rim_ref[c * 10 + l].astype(f32) + gain_ref[l] * field[16:24, :]
            scaled[l, 0:16, :] = decay_ref[c * 10 + l] * own
            scaled[l, 16:24, :] = decay_ref[c * 10 + l] * rim
        for l in range(1, 9):
            value = advect(mix(scaled, l, l), l - 1)
            if 2 <= l < 8:
                total = total + profile_ref[c * 6 + l - 2] * value[0:16]
            later[l - 1] = decay_ref[c * 10 + l] * value
        for q in range(groups):
            surface_ref[q, pl.ds(c * 16, 16), :] = total[:, q * 128 : (q + 1) * 128]
        for l in range(2, 8):
            out_ref[c, l - 2] = advect(mix(later, l - 1, l), l - 1)[0:16]
        return 0

    lax.fori_loop(0, lam_ref.shape[0], tracer, 0)


def on_device(
    lam_in,
    courant_x,
    courant_y,
    kz_face,
    loss_rate,
    profile,
    kernel,
    obs_values,
    obs_tile,
    obs_block,
):
    f32, bf16 = jnp.float32, jnp.bfloat16
    size_x, size_core, size_z, size_y = SPLIT
    lev_count, tile_count = size_x * size_core, size_z * size_y
    members = lev_count * size_y
    lev_index, tile_index = lax.axis_index(LEV), lax.axis_index(TILE)
    z_index = lax.axis_index("z")
    tracers, levels, rows, cols = lam_in.shape
    blocks = rows * cols // 128
    vmem = pl.BlockSpec(memory_space=pltpu.VMEM)
    smem = pl.BlockSpec(memory_space=pltpu.SMEM)
    params = pltpu.CompilerParams(vmem_limit_bytes=VMEM)

    last_row = (tile_index == tile_count - 1) & (jnp.arange(rows) == rows - 1)
    cx = jnp.where(last_row[None, :, None], 0.0, courant_x)
    cy = jnp.where((jnp.arange(cols) == cols - 1)[None, None, :], 0.0, courant_y)
    top = (lev_index == lev_count - 1) & (jnp.arange(levels) == levels - 1)
    kz = jnp.where(top[:, None, None], 0.0, kz_face)
    decay = jnp.exp(-loss_rate)

    def coded(first):
        row = jnp.concatenate([decay[:, first : first + 2].reshape(-1), kernel[first : first + 2]])
        row = jnp.pad(row, (0, cols - row.shape[0]))
        head = lax.reduce_precision(row, 8, 7)
        both = jnp.stack([head, row - head])
        return jnp.pad(both, ((0, rows - 2), (0, 0)))[None]

    def planes(first):
        return lam_in[:, first : first + 2].reshape(2 * tracers, rows, cols)

    up = jnp.concatenate([planes(levels - 2), kz[-2:], cx[-1:], cy[-1:], coded(levels - 2)])
    down = jnp.concatenate([planes(0), kz[:1], cx[:1], cy[:1], coded(0)])
    low = chain(LEV, lev_count, 1)(up.astype(bf16))
    high = chain(LEV, lev_count, -1)(down.astype(bf16))

    place = {d: (k, j) for k, pair in enumerate(SHIFTS) for j, d in enumerate(pair)}
    order = jnp.array([2 * size_y * place[d][0] + place[d][1] for d in range(size_z)], jnp.int32)
    tile = jnp.arange(tile_count)
    distance = (tile // size_y - z_index + size_z) % size_z
    base = (CAP * (order[distance] + 2 * (tile % size_y))).astype(f32)[:, None]
    packed = pl.pallas_call(
        pack_kernel,
        out_shape=jax.ShapeDtypeStruct((members, 2 * CAP + 16, 128), bf16),
        in_specs=[vmem] * 4,
        out_specs=vmem,
        compiler_params=params,
    )(obs_tile.reshape(1, -1), obs_block.reshape(1, -1), base, obs_values)
    got = lax.all_to_all(packed, LEV + ("y",), 0, 0, tiled=True)
    sums = pl.pallas_call(
        sum_kernel,
        out_shape=jax.ShapeDtypeStruct((2, blocks, 128), f32),
        in_specs=[vmem],
        out_specs=vmem,
        compiler_params=params,
    )(got)

    def along_z(value, j):
        perm = [
            (k * size_z + z, k * size_z + (z + SHIFTS[k][j]) % size_z)
            for k in range(lev_count)
            for z in range(size_z)
        ]
        return lax.ppermute(value, LEV + ("z",), perm)

    part = along_z(sums[0], 0) + along_z(sums[1], 1)
    edge = 2 * cols // 128
    after = chain(TILE, tile_count, -1)(part[:edge])
    prior = chain(TILE, tile_count, 1)(part[-edge:])
    part = jnp.concatenate([part, after, prior])
    parts = lax.all_gather(part, LEV, axis=0)

    def extended(own, below, above):
        return jnp.concatenate([below.astype(f32), own, above.astype(f32)], axis=-3)

    low_lam = low[: 2 * tracers].reshape(tracers, 2, rows, cols)
    high_lam = high[: 2 * tracers].reshape(tracers, 2, rows, cols)
    edge_of = lambda a, first, n: lax.slice_in_dim(a, first, first + n, axis=a.ndim - 2)

    def rim(first, n):
        cut = lambda a: edge_of(a, first, n)
        lam_rim = extended(cut(lam_in), cut(low_lam), cut(high_lam))
        kz_rim = extended(cut(kz), cut(low[8:10]), cut(high[8:9]))
        cx_rim = extended(cut(cx), cut(low[10:11]), cut(high[9:10]))
        cy_rim = extended(cut(cy), cut(low[11:12]), cut(high[10:11]))
        lam_rim = lam_rim.reshape((-1,) + lam_rim.shape[2:])
        return jnp.concatenate([lam_rim, kz_rim, cx_rim, cy_rim]).astype(bf16)

    from_after = chain(TILE, tile_count, -1)(rim(0, 2))
    from_prior = chain(TILE, tile_count, 1)(rim(rows - 2, 2))
    gap = jnp.zeros((from_after.shape[0], 4, cols), bf16)
    rims = jnp.concatenate([from_after, gap, from_prior], axis=1)

    def decoded(row):
        both = row[:2, : 2 * tracers + 2].astype(f32)
        both = both[0] + both[1]
        return both[: 2 * tracers].reshape(tracers, 2), both[2 * tracers :]

    low_decay, low_gain = decoded(low[12])
    high_decay, high_gain = decoded(high[11])
    decays = jnp.concatenate([low_decay, decay, high_decay], axis=1).reshape(-1)
    gains = jnp.concatenate([low_gain, kernel, high_gain])

    lam_out, surface = pl.pallas_call(
        step_kernel,
        out_shape=(
            jax.ShapeDtypeStruct(lam_in.shape, f32),
            jax.ShapeDtypeStruct((lev_count, tracers * rows, cols // lev_count), f32),
        ),
        in_specs=[smem] * 3 + [vmem] * 8,
        out_specs=(vmem, vmem),
        scratch_shapes=[
            pltpu.VMEM((9, ROWS, cols), f32),
            pltpu.VMEM((8, ROWS, cols), f32),
            pltpu.VMEM((8, ROWS, cols), f32),
            pltpu.VMEM((ROWS * cols // 128, 128), f32),
            pltpu.VMEM((ROWS, cols), f32),
            pltpu.VMEM((10, ROWS, cols), f32),
            pltpu.VMEM((8, ROWS, cols), f32),
            pltpu.VMEM((ROWS, cols), f32),
            pltpu.VMEM((ROWS, cols), f32),
        ],
        compiler_params=params,
    )(
        decays,
        gains,
        profile.reshape(-1),
        lam_in,
        kz,
        cx,
        cy,
        low,
        high,
        rims,
        parts,
    )
    shares = lax.all_to_all(surface, LEV, 0, 0, tiled=True)
    gradient = jnp.sum(shares, axis=0).reshape(tracers, rows, cols // lev_count)
    return lam_out, gradient


def solution(mesh):
    grid = Mesh(np.asarray(mesh.devices).reshape(SPLIT), ("x", "core", "z", "y"))
    in_specs = (
        P(None, LEV, TILE, None),
        P(LEV, TILE, None),
        P(LEV, TILE, None),
        P(LEV, TILE, None),
        P(None, LEV),
        P(None, LEV),
        P(LEV),
        P(LEV + TILE, None),
        P(LEV + TILE, None),
        P(LEV + TILE),
    )
    out_specs = (P(None, LEV, TILE, None), P(None, TILE, LEV))
    return jax.shard_map(
        on_device, mesh=grid, in_specs=in_specs, out_specs=out_specs, check_vma=False
    )
```

```python
import functools

import jax
import jax.numpy as jnp
import numpy as np
from jax import lax
from jax.experimental import pallas as pl
from jax.experimental.pallas import tpu as pltpu
from jax.sharding import Mesh
from jax.sharding import PartitionSpec as P

SPLIT = (4, 2, 16, 4)
SHIFTS = ((0, 8), (4, 12), (1, 9), (7, 15), (2, 10), (6, 14), (3, 11), (5, 13))
CAP = 64
LEV = ("x", "core")
TILE = ("z", "y")
ROWS = 24
STRIP = 144
VMEM = 24 * 1024 * 1024
F32, BF16 = jnp.float32, jnp.bfloat16


def chain(axes, count, steps):
    first, last = max(0, -steps), min(count, count - steps)
    return functools.partial(
        lax.ppermute, axis_name=axes, perm=[(i, i + steps) for i in range(first, last)]
    )


def iota(shape, dim):
    return lax.broadcasted_iota(jnp.int32, shape, dim)


def pack_kernel(where_ref, tile_ref, block_ref, obs_ref, out_ref):
    size_z, size_y = SPLIT[2:]
    tiles = size_z * size_y
    members, depth, _ = out_ref.shape
    count = obs_ref.shape[0]
    pair, part = 2 * CAP, 256
    tile = tile_ref[...]
    block = block_ref[...]
    t = iota((tiles, 1), 0)
    distance = t // size_y - where_ref[0]
    distance = jnp.where(distance < 0, distance + size_z, distance)
    order = 2 * (t % size_y)
    for k, both in enumerate(SHIFTS):
        for j, d in enumerate(both):
            order = order + jnp.where(distance == d, 2 * size_y * k + j, 0)
    start = (CAP * order).astype(F32)
    hot = (iota((tiles, count), 0) == tile).astype(F32)
    cuts = [hot[:, i : i + part] for i in range(0, count, part)]
    before = (iota((part, part), 0) < iota((part, part), 1)).astype(BF16)
    rank = jnp.dot(
        jnp.concatenate(cuts, axis=0).astype(BF16), before, preferred_element_type=F32
    )
    places = []
    for i, cut in enumerate(cuts):
        here = cut * (rank[i * tiles : (i + 1) * tiles] + start)
        places.append(jnp.sum(here, axis=0, keepdims=True))
        start = start + jnp.sum(cut, axis=1, keepdims=True)
    place = jnp.concatenate(places, axis=1).astype(jnp.int32)
    member = place // pair
    slot = place - member * pair
    code = (block + 1 + jnp.where(slot >= CAP, 128, 0)).astype(F32)
    owns = (iota((members, count), 0) == member).astype(F32)
    at = iota((pair, count), 0) == slot
    codes = lax.dot_general(
        owns.astype(BF16),
        jnp.where(at, code, 0.0).astype(BF16),
        (((1,), (1,)), ((), ())),
        preferred_element_type=F32,
    ).astype(BF16)
    out_ref[:, pair:, :] = jnp.broadcast_to(codes[:, None, :], (members, depth - pair, 128))
    slots = at.astype(F32).astype(BF16)
    group = 4
    for g in range(0, members, group):
        pick = jnp.concatenate(
            [slots * owns[m : m + 1].astype(BF16) for m in range(g, g + group)], axis=0
        )
        got = jnp.dot(pick, obs_ref[...], preferred_element_type=F32).astype(BF16)
        out_ref[g : g + group, :pair, :] = got.reshape(group, pair, 128)


def sum_kernel(got_ref, out_ref):
    sources = got_ref.shape[0]
    pair = 2 * CAP
    total = jnp.zeros((256, 128), F32)
    for s in range(0, sources, 2):
        code = jnp.concatenate(
            [got_ref[s + i, pair : pair + 16, :].astype(F32)[:1] for i in range(2)], axis=1
        )
        pick = iota((256, 2 * pair), 0) + 1 == code.astype(jnp.int32)
        rows = jnp.concatenate([got_ref[s + i, :pair, :] for i in range(2)], axis=0)
        total += jnp.dot(pick.astype(BF16), rows, preferred_element_type=F32)
    out_ref[...] = total.reshape(2, 128, 128)


def masks(where_ref):
    def kz(value, level):
        return jnp.where(where_ref[2] == 1, 0.0, value) if level == 5 else value

    def cx(value, first):
        last = iota(value.shape, 0) + first == 15
        return jnp.where(last & (where_ref[1] == 1), 0.0, value)

    def cy(value):
        return jnp.where(iota(value.shape, 1) == value.shape[1] - 1, 0.0, value)

    return kz, cx, cy


def level_kernel(
    where_ref, decay_ref, gain_ref, lam_ref, kz_ref, cx_ref, cy_ref, after_ref, up_ref, down_ref
):
    mask_kz, mask_cx, mask_cy = masks(where_ref)
    for ref, first in ((up_ref, 4), (down_ref, 0)):
        for c in range(4):
            for i in range(2):
                ref[c * 2 + i] = lam_ref[c, first + i].astype(BF16)
        levels = (4, 5) if first else (0,)
        for i, level in enumerate(levels):
            ref[8 + i] = mask_kz(kz_ref[level], level).astype(BF16)
        at = 8 + len(levels)
        ref[at] = mask_cx(cx_ref[levels[-1]], 0).astype(BF16)
        ref[at + 1] = mask_cy(cy_ref[levels[-1]]).astype(BF16)
        row = iota(ref.shape[1:], 0)
        plane = jnp.zeros(ref.shape[1:], F32)
        for i in range(2):
            plane = jnp.where(row == 8 + i, gain_ref[first + i], plane)
            for c in range(4):
                plane = jnp.where(row == c * 2 + i, decay_ref[c * 6 + first + i], plane)
        rough = plane.astype(BF16)
        ref[at + 2] = rough
        ref[at + 3] = (plane - rough.astype(F32)).astype(BF16)


def row_kernel(
    where_ref, lam_ref, kz_ref, cx_ref, cy_ref, low_ref, high_ref, prior_ref, next_ref, strip
):
    mask_kz, mask_cx, mask_cy = masks(where_ref)
    for ref, first in ((prior_ref, 0), (next_ref, 14)):
        rows = slice(first, first + 2)

        def put(plane, value):
            strip[2 * plane : 2 * plane + 2, :] = value

        strip[130:144, :] = jnp.zeros((14, strip.shape[1]), F32)
        for c in range(4):
            for l in range(10):
                if l < 2:
                    value = low_ref[c * 2 + l].astype(F32)[rows]
                elif l < 8:
                    value = lam_ref[c, l - 2, rows, :]
                else:
                    value = high_ref[c * 2 + l - 8].astype(F32)[rows]
                put(c * 10 + l, value)
        for l in range(9):
            if l < 2:
                value = low_ref[8 + l].astype(F32)[rows]
            elif l < 8:
                value = mask_kz(kz_ref[l - 2, rows, :], l - 2)
            else:
                value = high_ref[8].astype(F32)[rows]
            put(40 + l, value)
        for l in range(8):
            if l < 1:
                x, y = low_ref[10].astype(F32)[rows], low_ref[11].astype(F32)[rows]
            elif l < 7:
                x = mask_cx(cx_ref[l - 1, rows, :], first)
                y = mask_cy(cy_ref[l - 1, rows, :])
            else:
                x, y = high_ref[9].astype(F32)[rows], high_ref[10].astype(F32)[rows]
            put(49 + l, x)
            put(57 + l, y)
        ref[...] = strip[...].astype(BF16)


def ready_kernel(
    where_ref,
    decay_ref,
    gain_ref,
    profile_ref,
    lam_ref,
    kz_ref,
    cx_ref,
    cy_ref,
    low_ref,
    high_ref,
    after_ref,
    prior_ref,
    kzs,
    cxs,
    cys,
    mixed_ref,
    coef_ref,
    surface_ref,
    decays,
    strip_after,
    strip_prior,
    gains,
    scaled,
):
    mask_kz, mask_cx, mask_cy = masks(where_ref)
    cols = lam_ref.shape[3]
    strip_after[...] = after_ref[...].astype(F32)
    strip_prior[...] = prior_ref[...].astype(F32)

    def rim(ref, plane):
        if ref.shape[0] == ROWS:
            ref[16:24, :] = jnp.zeros((8, cols), F32)
            ref[16:18, :] = strip_after[2 * plane : 2 * plane + 2, :]
            ref[22:24, :] = strip_prior[2 * plane : 2 * plane + 2, :]

    for l in range(9):
        if l < 2:
            body = low_ref[8 + l].astype(F32)
        elif l < 8:
            body = mask_kz(kz_ref[l - 2], l - 2)
        else:
            body = high_ref[8].astype(F32)
        kzs[l, 0:16, :] = body
        rim(kzs.at[l], 40 + l)
    for l in range(8):
        if l < 1:
            x, y = low_ref[10].astype(F32), low_ref[11].astype(F32)
        elif l < 7:
            x, y = mask_cx(cx_ref[l - 1], 0), mask_cy(cy_ref[l - 1])
        else:
            x, y = high_ref[9].astype(F32), high_ref[10].astype(F32)
        cxs[l, 0:16, :] = x
        cys[l, 0:16, :] = y
        rim(cxs.at[l], 49 + l)
        rim(cys.at[l], 57 + l)
    low_row = low_ref[12].astype(F32) + low_ref[13].astype(F32)
    high_row = high_ref[11].astype(F32) + high_ref[12].astype(F32)
    for l in range(10):
        for c in range(4):
            at = slice(c * 10 + l, c * 10 + l + 1)
            if l < 2:
                decays[at, :] = low_row[c * 2 + l : c * 2 + l + 1]
            elif l < 8:
                decays[at, :] = jnp.full((1, cols), decay_ref[c * 6 + l - 2], F32)
            else:
                decays[at, :] = high_row[c * 2 + l - 8 : c * 2 + l - 7]
        if l < 2:
            gains[l : l + 1, :] = low_row[8 + l : 9 + l]
        elif l < 8:
            gains[l : l + 1, :] = jnp.full((1, cols), gain_ref[l - 2], F32)
        else:
            gains[l : l + 1, :] = high_row[l : l + 1]
    for c in range(4):
        total = jnp.zeros((16, cols), F32)
        for l in range(10):
            if l < 2:
                body = low_ref[c * 2 + l].astype(F32)
            elif l < 8:
                body = lam_ref[c, l - 2]
                total = total + profile_ref[c * 6 + l - 2] * body
            else:
                body = high_ref[c * 2 + l - 8].astype(F32)
            scaled[l, 0:16, :] = body
            rim(scaled.at[l], c * 10 + l)
            scaled[l] = scaled[l] * decays[c * 10 + l : c * 10 + l + 1, :]
        surface_ref[c] = total

        def both(l):
            at = c * 10 + l
            return decays[at : at + 1, :] * gains[l : l + 1, :]

        for l in range(1, 9):
            here = scaled[l]
            above, below = kzs[l], kzs[l - 1]
            mixed_ref[c, l - 1] = (
                here + above * (scaled[l + 1] - here) - below * (here - scaled[l - 1])
            )
            gain = both(l)
            coef_ref[c, l - 1] = (
                gain + above * (both(l + 1) - gain) - below * (gain - both(l - 1))
            )


def roll(x, shift, axis):
    return pltpu.roll(x, shift % x.shape[axis], axis)


def advect(m, cx, cy, rows):
    gx = roll(m, -1, 0) - m
    back = roll(jnp.minimum(cx, 0.0) * gx, 1, 0)
    value = m[:rows] + jnp.maximum(cx[:rows], 0.0) * gx[:rows] + back[:rows]
    m, cy = m[:rows], cy[:rows]
    gy = roll(m, -1, 1) - m
    return value + jnp.maximum(cy, 0.0) * gy + roll(jnp.minimum(cy, 0.0) * gy, 1, 1)


def first_kernel(
    gain_ref,
    profile_ref,
    cxs,
    cys,
    mixed_ref,
    coef_ref,
    early_ref,
    decays,
    map_ref,
    later_ref,
    surface_ref,
    blocks,
    field,
):
    cols = early_ref.shape[2]
    groups, parts = cols // 128, map_ref.shape[0]
    total = map_ref[0]
    for k in range(1, parts):
        total = total + map_ref[k]
    blocks[0:144, :] = total[0:144]
    blocks[144:176, :] = jnp.zeros((32, 128), F32)
    blocks[176:192, :] = total[144:160]
    for q in range(groups):
        field[:, q * 128 : (q + 1) * 128] = blocks[pl.ds(q, ROWS, stride=groups), :]

    def tracer(c, _):
        weight = 0.0
        for l in range(6):
            weight = weight + profile_ref[c * 6 + l] * gain_ref[l]
        total = early_ref[c] + weight * field[0:16, :]
        for l in range(8):
            m = mixed_ref[c, l] + coef_ref[c, l] * field[...]
            value = advect(m, cxs[l], cys[l], ROWS)
            if 1 <= l < 7:
                total = total + profile_ref[c * 6 + l - 1] * value[0:16]
            later_ref[c, l] = decays[pl.ds(c * 10 + l + 1, 1), :] * value
        for q in range(groups):
            surface_ref[q, pl.ds(c * 16, 16), :] = total[:, q * 128 : (q + 1) * 128]
        return 0

    lax.fori_loop(0, early_ref.shape[0], tracer, 0)


def second_kernel(kzs, cxs, cys, later_ref, out_ref):
    def tracer(c, _):
        for l in range(6):
            here = later_ref[c, l + 1]
            m = (
                here
                + kzs[l + 2] * (later_ref[c, l + 2] - here)
                - kzs[l + 1] * (here - later_ref[c, l])
            )
            out_ref[c, l] = advect(m, cxs[l + 1], cys[l + 1], 16)
        return 0

    lax.fori_loop(0, out_ref.shape[0], tracer, 0)


def on_device(
    lam_in,
    courant_x,
    courant_y,
    kz_face,
    loss_rate,
    profile,
    kernel,
    obs_values,
    obs_tile,
    obs_block,
):
    size_x, size_core, size_z, size_y = SPLIT
    lev_count, tile_count = size_x * size_core, size_z * size_y
    members = lev_count * size_y
    tracers, levels, rows, cols = lam_in.shape
    blocks = rows * cols // 128
    vmem = pl.BlockSpec(memory_space=pltpu.VMEM)
    smem = pl.BlockSpec(memory_space=pltpu.SMEM)
    anywhere = pl.BlockSpec(memory_space=pl.ANY)
    shape = jax.ShapeDtypeStruct

    def call(body, outs, specs, scratch=(), flops=0, moved=0):
        return pl.pallas_call(
            body,
            out_shape=outs,
            in_specs=specs,
            out_specs=jax.tree.map(lambda _: vmem, outs),
            scratch_shapes=[pltpu.VMEM(s, F32) for s in scratch],
            compiler_params=pltpu.CompilerParams(vmem_limit_bytes=VMEM),
            cost_estimate=pl.CostEstimate(flops=flops, bytes_accessed=moved, transcendentals=0),
        )

    where = jnp.stack(
        [
            lax.axis_index("z"),
            (lax.axis_index(TILE) == tile_count - 1).astype(jnp.int32),
            (lax.axis_index(LEV) == lev_count - 1).astype(jnp.int32),
        ]
    )
    decay = jnp.exp(-loss_rate).reshape(-1)
    weights = profile.reshape(-1)

    packed = call(
        pack_kernel,
        shape((members, 2 * CAP + 16, 128), BF16),
        [smem] + [vmem] * 3,
        flops=1 << 30,
        moved=2 << 20,
    )(where, obs_tile.reshape(1, -1), obs_block.reshape(1, -1), obs_values)
    got = lax.all_to_all(packed, LEV + ("y",), 0, 0, tiled=True)

    up, down = call(
        level_kernel,
        (shape((14, rows, cols), BF16), shape((13, rows, cols), BF16)),
        [smem] * 3 + [vmem] * 4 + [anywhere],
        moved=4 << 20,
    )(where, decay, kernel, lam_in, kz_face, courant_x, courant_y, packed)
    low = chain(LEV, lev_count, 1)(up)
    high = chain(LEV, lev_count, -1)(down)
    first_rows, last_rows = call(
        row_kernel,
        (shape((STRIP, cols), BF16), shape((STRIP, cols), BF16)),
        [smem] + [vmem] * 6,
        scratch=[(STRIP, cols)],
        moved=5 << 20,
    )(where, lam_in, kz_face, courant_x, courant_y, low, high)
    after = chain(TILE, tile_count, -1)(first_rows)
    prior = chain(TILE, tile_count, 1)(last_rows)
    kzs, cxs, cys, mixed, coef, early, decays = call(
        ready_kernel,
        (
            shape((9, ROWS, cols), F32),
            shape((8, ROWS, cols), F32),
            shape((8, ROWS, cols), F32),
            shape((tracers, 8, ROWS, cols), F32),
            shape((tracers, 8, ROWS, cols), F32),
            shape((tracers, rows, cols), F32),
            shape((10 * tracers, cols), F32),
        ),
        [smem] * 4 + [vmem] * 8,
        scratch=[(STRIP, cols), (STRIP, cols), (16, cols), (10, ROWS, cols)],
        moved=12 << 20,
    )(
        where,
        decay,
        kernel,
        weights,
        lam_in,
        kz_face,
        courant_x,
        courant_y,
        low,
        high,
        after,
        prior,
    )

    sums = call(
        sum_kernel, shape((2, blocks, 128), F32), [vmem], flops=1 << 28, moved=1 << 20
    )(got)

    def along_z(value, j):
        perm = [
            (k * size_z + z, k * size_z + (z + SHIFTS[k][j]) % size_z)
            for k in range(lev_count)
            for z in range(size_z)
        ]
        return lax.ppermute(value, LEV + ("z",), perm)

    part = along_z(sums[0], 0) + along_z(sums[1], 1)
    edge = 2 * cols // 128
    part_after = chain(TILE, tile_count, -1)(part[:edge])
    part_prior = chain(TILE, tile_count, 1)(part[-edge:])
    parts = lax.all_gather(jnp.concatenate([part, part_after, part_prior]), LEV, axis=0)

    later, surface = call(
        first_kernel,
        (
            shape((tracers, 8, ROWS, cols), F32),
            shape((lev_count, tracers * rows, cols // lev_count), F32),
        ),
        [smem] * 2 + [vmem] * 7,
        scratch=[(ROWS * cols // 128, 128), (ROWS, cols)],
        moved=8 << 20,
    )(kernel, weights, cxs, cys, mixed, coef, early, decays, parts)
    shares = lax.all_to_all(surface, LEV, 0, 0, tiled=True)
    lam_out = call(
        second_kernel, shape(lam_in.shape, F32), [vmem] * 4, moved=6 << 20
    )(kzs, cxs, cys, later)
    gradient = jnp.sum(shares, axis=0).reshape(tracers, rows, cols // lev_count)
    return lam_out, gradient


def solution(mesh):
    grid = Mesh(np.asarray(mesh.devices).reshape(SPLIT), ("x", "core", "z", "y"))
    in_specs = (
        P(None, LEV, TILE, None),
        P(LEV, TILE, None),
        P(LEV, TILE, None),
        P(LEV, TILE, None),
        P(None, LEV),
        P(None, LEV),
        P(LEV),
        P(LEV + TILE, None),
        P(LEV + TILE, None),
        P(LEV + TILE),
    )
    out_specs = (P(None, LEV, TILE, None), P(None, TILE, LEV))
    return jax.shard_map(
        on_device, mesh=grid, in_specs=in_specs, out_specs=out_specs, check_vma=False
    )
```

```python
import functools

import jax
import jax.numpy as jnp
import numpy as np
from jax import lax
from jax.experimental import pallas as pl
from jax.experimental.pallas import tpu as pltpu
from jax.sharding import Mesh
from jax.sharding import PartitionSpec as P

SPLIT = (4, 2, 16, 4)
SHIFTS = ((0, 8), (4, 12), (1, 9), (7, 15), (2, 10), (6, 14), (3, 11), (5, 13))
CAP = 64
LEV = ("x", "core")
TILE = ("z", "y")
ROWS = 24
STRIP = 144
VMEM = 24 * 1024 * 1024
MOST = 63487488
F32, BF16 = jnp.float32, jnp.bfloat16


def chain(axes, count, steps):
    first, last = max(0, -steps), min(count, count - steps)
    return functools.partial(
        lax.ppermute, axis_name=axes, perm=[(i, i + steps) for i in range(first, last)]
    )


def iota(shape, dim):
    return lax.broadcasted_iota(jnp.int32, shape, dim)


def rank_of(tile, here, size_z, size_y):
    distance = tile // size_y - here
    distance = jnp.where(distance < 0, distance + size_z, distance)
    order = 2 * (tile % size_y)
    for k, both in enumerate(SHIFTS):
        for j, d in enumerate(both):
            order = order + jnp.where(distance == d, 2 * size_y * k + j, 0)
    return order


def one(mask):
    return mask.astype(F32).astype(BF16)


def pack_kernel(
    where_ref,
    tile_hbm,
    block_hbm,
    obs_hbm,
    out_ref,
    tile_ref,
    block_ref,
    obs_ref,
    ordered,
    starts,
    starts_smem,
    sems,
):
    size_z, size_y = SPLIT[2:]
    tiles = size_z * size_y
    members, depth, _ = out_ref.shape
    count = obs_ref.shape[0]
    pair, part = 2 * CAP, 256
    copies = [
        pltpu.make_async_copy(tile_hbm, tile_ref, sems.at[0]),
        pltpu.make_async_copy(block_hbm, block_ref, sems.at[1]),
        pltpu.make_async_copy(obs_hbm, obs_ref, sems.at[2]),
    ]
    for copy in copies:
        copy.start()
    order = rank_of(iota((tiles, 1), 0), where_ref[0], size_z, size_y)
    order_row = rank_of(iota((1, tiles), 1), where_ref[0], size_z, size_y)
    before = (iota((part, part), 0) < iota((part, part), 1)).astype(BF16)
    copies[0].wait()
    hot = (iota((tiles, count), 0) == tile_ref[...]).astype(F32)
    cuts = [hot[:, i : i + part] for i in range(0, count, part)]
    counts = [jnp.sum(cut, axis=1, keepdims=True) for cut in cuts]
    amount = counts[0]
    for more in counts[1:]:
        amount = amount + more
    amounts = jnp.broadcast_to(amount, (tiles, 128)).astype(BF16)
    first = jnp.dot(one(order_row < order), amounts, preferred_element_type=F32)[:, :1]
    opening = jnp.dot(one(order_row // 2 < order // 2), amounts, preferred_element_type=F32)[:, :1]
    ahead = jnp.where(order < 2 * iota((tiles, 128), 1), amount, 0.0)
    ahead = jnp.sum(ahead, axis=0, keepdims=True)
    starts[...] = jnp.broadcast_to(ahead, (8, 128)).astype(jnp.int32)
    sent = pltpu.make_async_copy(starts, starts_smem, sems.at[3])
    sent.start()
    rank = jnp.dot(
        jnp.concatenate(cuts, axis=0).astype(BF16), before, preferred_element_type=F32
    )
    tag = (pair * order).astype(F32)
    places, slots = [], []
    for i, cut in enumerate(cuts):
        at = rank[i * tiles : (i + 1) * tiles] + first
        places.append(jnp.sum(cut * at, axis=0, keepdims=True))
        slots.append(jnp.sum(cut * (at - opening + tag), axis=0, keepdims=True))
        first = first + counts[i]
    place = jnp.concatenate(places, axis=1).astype(jnp.int32)
    slot = jnp.concatenate(slots, axis=1).astype(jnp.int32)
    tile_order = slot // pair
    slot = slot - tile_order * pair
    copies[1].wait()
    code = (block_ref[...] + 1 + 128 * (tile_order % 2)).astype(F32)
    codes = lax.dot_general(
        one(iota((members, count), 0) == tile_order // 2),
        jnp.where(iota((pair, count), 0) == slot, code, 0.0).astype(BF16),
        (((1,), (1,)), ((), ())),
        preferred_element_type=F32,
    ).astype(BF16)
    out_ref[:, pair:, :] = jnp.broadcast_to(codes[:, None, :], (members, depth - pair, 128))
    copies[2].wait()
    for i in range(0, count, part):
        pick = one(iota((part, count), 0) + i == place)
        ordered[i : i + part, :] = jnp.dot(pick, obs_ref[...], preferred_element_type=F32)
    ordered[count : count + pair, :] = jnp.zeros((pair, 128), F32)
    sent.wait()
    for m in range(members):
        rows = ordered[pl.ds(starts_smem[0, m], pair), :]
        out_ref[m, :pair, :] = rows.astype(BF16)


def sum_kernel(got_ref, out_ref):
    sources = got_ref.shape[0]
    pair = 2 * CAP
    total = jnp.zeros((256, 128), F32)
    for s in range(0, sources, 2):
        code = jnp.concatenate(
            [got_ref[s + i, pair : pair + 16, :].astype(F32)[:1] for i in range(2)], axis=1
        )
        pick = iota((256, 2 * pair), 0) + 1 == code.astype(jnp.int32)
        rows = jnp.concatenate([got_ref[s + i, :pair, :] for i in range(2)], axis=0)
        total += jnp.dot(pick.astype(BF16), rows, preferred_element_type=F32)
    out_ref[...] = total.reshape(2, 128, 128)


def masks(where_ref):
    def kz(value, level):
        return jnp.where(where_ref[2] == 1, 0.0, value) if level == 5 else value

    def cx(value, first):
        last = iota(value.shape, 0) + first == 15
        return jnp.where(last & (where_ref[1] == 1), 0.0, value)

    def cy(value):
        return jnp.where(iota(value.shape, 1) == value.shape[1] - 1, 0.0, value)

    return kz, cx, cy


def level_kernel(
    where_ref, decay_ref, gain_ref, lam_ref, kz_ref, cx_ref, cy_ref, after_ref, up_ref, down_ref
):
    mask_kz, mask_cx, mask_cy = masks(where_ref)
    for ref, first in ((up_ref, 4), (down_ref, 0)):
        for c in range(4):
            for i in range(2):
                ref[c * 2 + i] = lam_ref[c, first + i].astype(BF16)
        levels = (4, 5) if first else (0,)
        for i, level in enumerate(levels):
            ref[8 + i] = mask_kz(kz_ref[level], level).astype(BF16)
        at = 8 + len(levels)
        ref[at] = mask_cx(cx_ref[levels[-1]], 0).astype(BF16)
        ref[at + 1] = mask_cy(cy_ref[levels[-1]]).astype(BF16)
        row = iota(ref.shape[1:], 0)
        plane = jnp.zeros(ref.shape[1:], F32)
        for i in range(2):
            plane = jnp.where(row == 8 + i, gain_ref[first + i], plane)
            for c in range(4):
                plane = jnp.where(row == c * 2 + i, decay_ref[c, first + i], plane)
        rough = plane.astype(BF16)
        ref[at + 2] = rough
        ref[at + 3] = (plane - rough.astype(F32)).astype(BF16)


def row_kernel(
    where_ref, lam_ref, kz_ref, cx_ref, cy_ref, low_ref, high_ref, prior_ref, next_ref, strip
):
    mask_kz, mask_cx, mask_cy = masks(where_ref)
    for ref, first in ((prior_ref, 0), (next_ref, 14)):
        rows = slice(first, first + 2)

        def put(plane, value):
            strip[2 * plane : 2 * plane + 2, :] = value

        strip[130:144, :] = jnp.zeros((14, strip.shape[1]), F32)
        for c in range(4):
            for l in range(10):
                if l < 2:
                    value = low_ref[c * 2 + l].astype(F32)[rows]
                elif l < 8:
                    value = lam_ref[c, l - 2, rows, :]
                else:
                    value = high_ref[c * 2 + l - 8].astype(F32)[rows]
                put(c * 10 + l, value)
        for l in range(9):
            if l < 2:
                value = low_ref[8 + l].astype(F32)[rows]
            elif l < 8:
                value = mask_kz(kz_ref[l - 2, rows, :], l - 2)
            else:
                value = high_ref[8].astype(F32)[rows]
            put(40 + l, value)
        for l in range(8):
            if l < 1:
                x, y = low_ref[10].astype(F32)[rows], low_ref[11].astype(F32)[rows]
            elif l < 7:
                x = mask_cx(cx_ref[l - 1, rows, :], first)
                y = mask_cy(cy_ref[l - 1, rows, :])
            else:
                x, y = high_ref[9].astype(F32)[rows], high_ref[10].astype(F32)[rows]
            put(49 + l, x)
            put(57 + l, y)
        ref[...] = strip[...].astype(BF16)


def ready_kernel(
    where_ref,
    decay_ref,
    gain_ref,
    profile_ref,
    lam_ref,
    kz_ref,
    cx_ref,
    cy_ref,
    low_ref,
    high_ref,
    after_ref,
    prior_ref,
    kzs,
    cxs,
    cys,
    mixed_ref,
    coef_ref,
    surface_ref,
    decays,
    strip_after,
    strip_prior,
    gains,
    scaled,
):
    mask_kz, mask_cx, mask_cy = masks(where_ref)
    cols = lam_ref.shape[3]
    strip_after[...] = after_ref[...].astype(F32)
    strip_prior[...] = prior_ref[...].astype(F32)

    def rim(ref, plane):
        if ref.shape[0] == ROWS:
            ref[16:24, :] = jnp.zeros((8, cols), F32)
            ref[16:18, :] = strip_after[2 * plane : 2 * plane + 2, :]
            ref[22:24, :] = strip_prior[2 * plane : 2 * plane + 2, :]

    for l in range(9):
        if l < 2:
            body = low_ref[8 + l].astype(F32)
        elif l < 8:
            body = mask_kz(kz_ref[l - 2], l - 2)
        else:
            body = high_ref[8].astype(F32)
        kzs[l, 0:16, :] = body
        rim(kzs.at[l], 40 + l)
    for l in range(8):
        if l < 1:
            x, y = low_ref[10].astype(F32), low_ref[11].astype(F32)
        elif l < 7:
            x, y = mask_cx(cx_ref[l - 1], 0), mask_cy(cy_ref[l - 1])
        else:
            x, y = high_ref[9].astype(F32), high_ref[10].astype(F32)
        cxs[l, 0:16, :] = x
        cys[l, 0:16, :] = y
        rim(cxs.at[l], 49 + l)
        rim(cys.at[l], 57 + l)
    low_row = low_ref[12].astype(F32) + low_ref[13].astype(F32)
    high_row = high_ref[11].astype(F32) + high_ref[12].astype(F32)
    for l in range(10):
        for c in range(4):
            at = slice(c * 10 + l, c * 10 + l + 1)
            if l < 2:
                decays[at, :] = low_row[c * 2 + l : c * 2 + l + 1]
            elif l < 8:
                decays[at, :] = jnp.full((1, cols), decay_ref[c, l - 2], F32)
            else:
                decays[at, :] = high_row[c * 2 + l - 8 : c * 2 + l - 7]
        if l < 2:
            gains[l : l + 1, :] = low_row[8 + l : 9 + l]
        elif l < 8:
            gains[l : l + 1, :] = jnp.full((1, cols), gain_ref[l - 2], F32)
        else:
            gains[l : l + 1, :] = high_row[l : l + 1]
    for c in range(4):
        total = jnp.zeros((16, cols), F32)
        for l in range(10):
            if l < 2:
                body = low_ref[c * 2 + l].astype(F32)
            elif l < 8:
                body = lam_ref[c, l - 2]
                total = total + profile_ref[c, l - 2] * body
            else:
                body = high_ref[c * 2 + l - 8].astype(F32)
            scaled[l, 0:16, :] = body
            rim(scaled.at[l], c * 10 + l)
            scaled[l] = scaled[l] * decays[c * 10 + l : c * 10 + l + 1, :]
        surface_ref[c] = total

        def both(l):
            at = c * 10 + l
            return decays[at : at + 1, :] * gains[l : l + 1, :]

        for l in range(1, 9):
            here = scaled[l]
            above, below = kzs[l], kzs[l - 1]
            mixed_ref[c, l - 1] = (
                here + above * (scaled[l + 1] - here) - below * (here - scaled[l - 1])
            )
            gain = both(l)
            coef_ref[c, l - 1] = (
                gain + above * (both(l + 1) - gain) - below * (gain - both(l - 1))
            )


def roll(x, shift, axis):
    return pltpu.roll(x, shift % x.shape[axis], axis)


def advect(m, cx, cy, rows):
    gx = roll(m, -1, 0) - m
    back = roll(jnp.minimum(cx, 0.0) * gx, 1, 0)
    value = m[:rows] + jnp.maximum(cx[:rows], 0.0) * gx[:rows] + back[:rows]
    m, cy = m[:rows], cy[:rows]
    gy = roll(m, -1, 1) - m
    return value + jnp.maximum(cy, 0.0) * gy + roll(jnp.minimum(cy, 0.0) * gy, 1, 1)


def first_kernel(
    gain_ref,
    profile_ref,
    cxs,
    cys,
    mixed_ref,
    coef_ref,
    early_ref,
    decays,
    map_ref,
    later_ref,
    surface_ref,
    blocks,
    field,
):
    cols = early_ref.shape[2]
    groups, parts = cols // 128, map_ref.shape[0]
    total = map_ref[0]
    for k in range(1, parts):
        total = total + map_ref[k]
    blocks[0:144, :] = total[0:144]
    blocks[144:176, :] = jnp.zeros((32, 128), F32)
    blocks[176:192, :] = total[144:160]
    for q in range(groups):
        field[:, q * 128 : (q + 1) * 128] = blocks[pl.ds(q, ROWS, stride=groups), :]

    def tracer(c, _):
        weight = 0.0
        for l in range(6):
            weight = weight + profile_ref[c, l] * gain_ref[l]
        total = early_ref[c] + weight * field[0:16, :]
        for l in range(8):
            m = mixed_ref[c, l] + coef_ref[c, l] * field[...]
            value = advect(m, cxs[l], cys[l], ROWS)
            if 1 <= l < 7:
                total = total + profile_ref[c, l - 1] * value[0:16]
            later_ref[c, l] = decays[pl.ds(c * 10 + l + 1, 1), :] * value
        for q in range(groups):
            surface_ref[q, pl.ds(c * 16, 16), :] = total[:, q * 128 : (q + 1) * 128]
        return 0

    lax.fori_loop(0, early_ref.shape[0], tracer, 0)


def second_kernel(kzs, cxs, cys, later_ref, out_ref):
    def tracer(c, _):
        for l in range(6):
            here = later_ref[c, l + 1]
            m = (
                here
                + kzs[l + 2] * (later_ref[c, l + 2] - here)
                - kzs[l + 1] * (here - later_ref[c, l])
            )
            out_ref[c, l] = advect(m, cxs[l + 1], cys[l + 1], 16)
        return 0

    lax.fori_loop(0, out_ref.shape[0], tracer, 0)


def on_device(
    lam_in,
    courant_x,
    courant_y,
    kz_face,
    loss_rate,
    profile,
    kernel,
    obs_values,
    obs_tile,
    obs_block,
):
    size_x, size_core, size_z, size_y = SPLIT
    lev_count, tile_count = size_x * size_core, size_z * size_y
    members = lev_count * size_y
    tracers, levels, rows, cols = lam_in.shape
    blocks = rows * cols // 128
    vmem = pl.BlockSpec(memory_space=pltpu.VMEM)
    smem = pl.BlockSpec(memory_space=pltpu.SMEM)
    anywhere = pl.BlockSpec(memory_space=pl.ANY)
    shape = jax.ShapeDtypeStruct

    def call(body, outs, specs, scratch=(), flops=0, moved=0, limit=VMEM):
        return pl.pallas_call(
            body,
            out_shape=outs,
            in_specs=specs,
            out_specs=jax.tree.map(lambda _: vmem, outs),
            scratch_shapes=[pltpu.VMEM(s, F32) if isinstance(s, tuple) else s for s in scratch],
            compiler_params=pltpu.CompilerParams(vmem_limit_bytes=limit),
            cost_estimate=pl.CostEstimate(flops=flops, bytes_accessed=moved, transcendentals=0),
        )

    where = jnp.stack(
        [
            lax.axis_index("z"),
            (lax.axis_index(TILE) == tile_count - 1).astype(jnp.int32),
            (lax.axis_index(LEV) == lev_count - 1).astype(jnp.int32),
        ]
    )
    decay = jnp.exp(-loss_rate)

    packed = call(
        pack_kernel,
        shape((members, 2 * CAP + 16, 128), BF16),
        [smem] + [anywhere] * 3,
        scratch=[
            pltpu.VMEM((1, obs_values.shape[0]), jnp.int32),
            pltpu.VMEM((1, obs_values.shape[0]), jnp.int32),
            pltpu.VMEM(obs_values.shape, BF16),
            (obs_values.shape[0] + 2 * CAP, 128),
            pltpu.VMEM((8, 128), jnp.int32),
            pltpu.SMEM((8, 128), jnp.int32),
            pltpu.SemaphoreType.DMA((4,)),
        ],
        flops=1 << 30,
        moved=2 << 20,
        limit=MOST,
    )(where, obs_tile.reshape(1, -1), obs_block.reshape(1, -1), obs_values)
    got = lax.all_to_all(packed, LEV + ("y",), 0, 0, tiled=True)

    up, down = call(
        level_kernel,
        (shape((14, rows, cols), BF16), shape((13, rows, cols), BF16)),
        [smem] * 3 + [vmem] * 4 + [anywhere],
        moved=4 << 20,
    )(where, decay, kernel, lam_in, kz_face, courant_x, courant_y, packed)
    low = chain(LEV, lev_count, 1)(up)
    high = chain(LEV, lev_count, -1)(down)
    first_rows, last_rows = call(
        row_kernel,
        (shape((STRIP, cols), BF16), shape((STRIP, cols), BF16)),
        [smem] + [vmem] * 6,
        scratch=[(STRIP, cols)],
        moved=5 << 20,
    )(where, lam_in, kz_face, courant_x, courant_y, low, high)
    after = chain(TILE, tile_count, -1)(first_rows)
    prior = chain(TILE, tile_count, 1)(last_rows)
    kzs, cxs, cys, mixed, coef, early, decays = call(
        ready_kernel,
        (
            shape((9, ROWS, cols), F32),
            shape((8, ROWS, cols), F32),
            shape((8, ROWS, cols), F32),
            shape((tracers, 8, ROWS, cols), F32),
            shape((tracers, 8, ROWS, cols), F32),
            shape((tracers, rows, cols), F32),
            shape((10 * tracers, cols), F32),
        ),
        [smem] * 4 + [vmem] * 8,
        scratch=[(STRIP, cols), (STRIP, cols), (16, cols), (10, ROWS, cols)],
        moved=12 << 20,
    )(
        where,
        decay,
        kernel,
        profile,
        lam_in,
        kz_face,
        courant_x,
        courant_y,
        low,
        high,
        after,
        prior,
    )

    sums = call(
        sum_kernel, shape((2, blocks, 128), F32), [vmem], flops=1 << 28, moved=1 << 20
    )(got)

    def along_z(value, j):
        perm = [
            (k * size_z + z, k * size_z + (z + SHIFTS[k][j]) % size_z)
            for k in range(lev_count)
            for z in range(size_z)
        ]
        return lax.ppermute(value, LEV + ("z",), perm)

    part = along_z(sums[0], 0) + along_z(sums[1], 1)
    edge = 2 * cols // 128
    part_after = chain(TILE, tile_count, -1)(part[:edge])
    part_prior = chain(TILE, tile_count, 1)(part[-edge:])
    parts = lax.all_gather(jnp.concatenate([part, part_after, part_prior]), LEV, axis=0)

    later, surface = call(
        first_kernel,
        (
            shape((tracers, 8, ROWS, cols), F32),
            shape((lev_count, tracers * rows, cols // lev_count), F32),
        ),
        [smem] * 2 + [vmem] * 7,
        scratch=[(ROWS * cols // 128, 128), (ROWS, cols)],
        moved=8 << 20,
    )(kernel, profile, cxs, cys, mixed, coef, early, decays, parts)
    shares = lax.all_to_all(surface, LEV, 0, 0, tiled=True)
    lam_out = call(
        second_kernel, shape(lam_in.shape, F32), [vmem] * 4, moved=6 << 20
    )(kzs, cxs, cys, later)
    gradient = jnp.sum(shares, axis=0).reshape(tracers, rows, cols // lev_count)
    return lam_out, gradient


def solution(mesh):
    grid = Mesh(np.asarray(mesh.devices).reshape(SPLIT), ("x", "core", "z", "y"))
    in_specs = (
        P(None, LEV, TILE, None),
        P(LEV, TILE, None),
        P(LEV, TILE, None),
        P(LEV, TILE, None),
        P(None, LEV),
        P(None, LEV),
        P(LEV),
        P(LEV + TILE, None),
        P(LEV + TILE, None),
        P(LEV + TILE),
    )
    out_specs = (P(None, LEV, TILE, None), P(None, TILE, LEV))
    return jax.shard_map(
        on_device, mesh=grid, in_specs=in_specs, out_specs=out_specs, check_vma=False
    )
```

```python
import functools

import jax
import jax.numpy as jnp
import numpy as np
from jax import lax
from jax.experimental import pallas as pl
from jax.experimental.pallas import tpu as pltpu
from jax.sharding import Mesh
from jax.sharding import PartitionSpec as P

SPLIT = (4, 2, 16, 4)
SHIFTS = ((0, 8), (1, 15), (2, 14), (7, 9), (3, 13), (6, 10), (4, 12), (5, 11))
CAP = 64
LEV = ("x", "core")
TILE = ("z", "y")
ROWS = 24
STRIP = 144
VMEM = 24 * 1024 * 1024
MOST = 63487488
F32, BF16 = jnp.float32, jnp.bfloat16


def chain(axes, count, steps):
    first, last = max(0, -steps), min(count, count - steps)
    return functools.partial(
        lax.ppermute, axis_name=axes, perm=[(i, i + steps) for i in range(first, last)]
    )


def iota(shape, dim):
    return lax.broadcasted_iota(jnp.int32, shape, dim)


def rank_of(tile, here, size_z, size_y):
    distance = tile // size_y - here
    distance = jnp.where(distance < 0, distance + size_z, distance)
    order = 2 * (tile % size_y)
    for k, both in enumerate(SHIFTS):
        for j, d in enumerate(both):
            order = order + jnp.where(distance == d, 2 * size_y * k + j, 0)
    return order


def one(mask):
    return mask.astype(F32).astype(BF16)


def pack_kernel(
    tile_hbm,
    block_hbm,
    obs_hbm,
    out_ref,
    tile_ref,
    block_ref,
    obs_ref,
    ordered,
    starts,
    starts_smem,
    sems,
):
    size_z, size_y = SPLIT[2:]
    tiles = size_z * size_y
    members, depth, _ = out_ref.shape
    count = obs_ref.shape[0]
    pair, part = 2 * CAP, 256
    copies = [
        pltpu.make_async_copy(tile_hbm, tile_ref, sems.at[0]),
        pltpu.make_async_copy(block_hbm, block_ref, sems.at[1]),
        pltpu.make_async_copy(obs_hbm, obs_ref, sems.at[2]),
    ]
    for copy in copies:
        copy.start()
    here = lax.axis_index("z")
    order = rank_of(iota((tiles, 1), 0), here, size_z, size_y)
    order_row = rank_of(iota((1, tiles), 1), here, size_z, size_y)
    before = (iota((part, part), 0) < iota((part, part), 1)).astype(BF16)
    copies[0].wait()
    hot = (iota((tiles, count), 0) == tile_ref[...]).astype(F32)
    cuts = [hot[:, i : i + part] for i in range(0, count, part)]
    counts = [jnp.sum(cut, axis=1, keepdims=True) for cut in cuts]
    amount = counts[0]
    for more in counts[1:]:
        amount = amount + more
    amounts = jnp.broadcast_to(amount, (tiles, 128)).astype(BF16)
    first = jnp.dot(one(order_row < order), amounts, preferred_element_type=F32)[:, :1]
    opening = jnp.dot(one(order_row // 2 < order // 2), amounts, preferred_element_type=F32)[:, :1]
    ahead = jnp.where(order < 2 * iota((tiles, 128), 1), amount, 0.0)
    ahead = jnp.sum(ahead, axis=0, keepdims=True)
    starts[...] = jnp.broadcast_to(ahead, (8, 128)).astype(jnp.int32)
    sent = pltpu.make_async_copy(starts, starts_smem, sems.at[3])
    sent.start()
    rank = jnp.dot(
        jnp.concatenate(cuts, axis=0).astype(BF16), before, preferred_element_type=F32
    )
    tag = (pair * order).astype(F32)
    places, slots = [], []
    for i, cut in enumerate(cuts):
        at = rank[i * tiles : (i + 1) * tiles] + first
        places.append(jnp.sum(cut * at, axis=0, keepdims=True))
        slots.append(jnp.sum(cut * (at - opening + tag), axis=0, keepdims=True))
        first = first + counts[i]
    place = jnp.concatenate(places, axis=1).astype(jnp.int32)
    slot = jnp.concatenate(slots, axis=1).astype(jnp.int32)
    tile_order = slot // pair
    slot = slot - tile_order * pair
    copies[1].wait()
    code = (block_ref[...] + 1 + 128 * (tile_order % 2)).astype(F32)
    codes = lax.dot_general(
        one(iota((members, count), 0) == tile_order // 2),
        jnp.where(iota((pair, count), 0) == slot, code, 0.0).astype(BF16),
        (((1,), (1,)), ((), ())),
        preferred_element_type=F32,
    ).astype(BF16)
    out_ref[:, pair:, :] = jnp.broadcast_to(codes[:, None, :], (members, depth - pair, 128))
    copies[2].wait()
    for i in range(0, count, part):
        pick = one(iota((part, count), 0) + i == place)
        ordered[i : i + part, :] = jnp.dot(pick, obs_ref[...], preferred_element_type=F32)
    ordered[count : count + pair, :] = jnp.zeros((pair, 128), F32)
    sent.wait()
    for m in range(members):
        rows = ordered[pl.ds(starts_smem[0, m], pair), :]
        out_ref[m, :pair, :] = rows.astype(BF16)


def sum_kernel(got_ref, out_ref):
    sources = got_ref.shape[0]
    pair = 2 * CAP
    total = jnp.zeros((256, 128), F32)
    for s in range(0, sources, 2):
        code = jnp.concatenate(
            [got_ref[s + i, pair : pair + 16, :].astype(F32)[:1] for i in range(2)], axis=1
        )
        pick = iota((256, 2 * pair), 0) + 1 == code.astype(jnp.int32)
        rows = jnp.concatenate([got_ref[s + i, :pair, :] for i in range(2)], axis=0)
        total += jnp.dot(pick.astype(BF16), rows, preferred_element_type=F32)
    out_ref[...] = total.reshape(2, 128, 128)


def masks(where_ref):
    def kz(value, level):
        return jnp.where(where_ref[1] == 1, 0.0, value) if level == 5 else value

    def cx(value, first):
        last = iota(value.shape, 0) + first == 15
        return jnp.where(last & (where_ref[0] == 1), 0.0, value)

    def cy(value):
        return jnp.where(iota(value.shape, 1) == value.shape[1] - 1, 0.0, value)

    return kz, cx, cy


def level_kernel(
    where_ref, decay_ref, gain_ref, lam_ref, kz_ref, cx_ref, cy_ref, after_ref, up_ref, down_ref
):
    mask_kz, mask_cx, mask_cy = masks(where_ref)
    for ref, first in ((up_ref, 4), (down_ref, 0)):
        for c in range(4):
            for i in range(2):
                ref[c * 2 + i] = lam_ref[c, first + i].astype(BF16)
        levels = (4, 5) if first else (0,)
        for i, level in enumerate(levels):
            ref[8 + i] = mask_kz(kz_ref[level], level).astype(BF16)
        at = 8 + len(levels)
        ref[at] = mask_cx(cx_ref[levels[-1]], 0).astype(BF16)
        ref[at + 1] = mask_cy(cy_ref[levels[-1]]).astype(BF16)
        row = iota(ref.shape[1:], 0)
        plane = jnp.zeros(ref.shape[1:], F32)
        for i in range(2):
            plane = jnp.where(row == 8 + i, gain_ref[first + i], plane)
            for c in range(4):
                plane = jnp.where(row == c * 2 + i, decay_ref[c, first + i], plane)
        rough = plane.astype(BF16)
        ref[at + 2] = rough
        ref[at + 3] = (plane - rough.astype(F32)).astype(BF16)


def row_kernel(
    where_ref, lam_ref, kz_ref, cx_ref, cy_ref, low_ref, high_ref, prior_ref, next_ref, strip
):
    mask_kz, mask_cx, mask_cy = masks(where_ref)
    for ref, first in ((prior_ref, 0), (next_ref, 14)):
        rows = slice(first, first + 2)

        def put(plane, value):
            strip[2 * plane : 2 * plane + 2, :] = value

        strip[130:144, :] = jnp.zeros((14, strip.shape[1]), F32)
        for c in range(4):
            for l in range(10):
                if l < 2:
                    value = low_ref[c * 2 + l].astype(F32)[rows]
                elif l < 8:
                    value = lam_ref[c, l - 2, rows, :]
                else:
                    value = high_ref[c * 2 + l - 8].astype(F32)[rows]
                put(c * 10 + l, value)
        for l in range(9):
            if l < 2:
                value = low_ref[8 + l].astype(F32)[rows]
            elif l < 8:
                value = mask_kz(kz_ref[l - 2, rows, :], l - 2)
            else:
                value = high_ref[8].astype(F32)[rows]
            put(40 + l, value)
        for l in range(8):
            if l < 1:
                x, y = low_ref[10].astype(F32)[rows], low_ref[11].astype(F32)[rows]
            elif l < 7:
                x = mask_cx(cx_ref[l - 1, rows, :], first)
                y = mask_cy(cy_ref[l - 1, rows, :])
            else:
                x, y = high_ref[9].astype(F32)[rows], high_ref[10].astype(F32)[rows]
            put(49 + l, x)
            put(57 + l, y)
        ref[...] = strip[...].astype(BF16)


def ready_kernel(
    where_ref,
    decay_ref,
    gain_ref,
    profile_ref,
    lam_ref,
    kz_ref,
    cx_ref,
    cy_ref,
    low_ref,
    high_ref,
    after_ref,
    prior_ref,
    kzs,
    cxs,
    cys,
    mixed_ref,
    coef_ref,
    surface_ref,
    decays,
    strip_after,
    strip_prior,
    gains,
    scaled,
):
    mask_kz, mask_cx, mask_cy = masks(where_ref)
    cols = lam_ref.shape[3]
    strip_after[...] = after_ref[...].astype(F32)
    strip_prior[...] = prior_ref[...].astype(F32)

    def rim(ref, plane):
        if ref.shape[0] == ROWS:
            ref[16:24, :] = jnp.zeros((8, cols), F32)
            ref[16:18, :] = strip_after[2 * plane : 2 * plane + 2, :]
            ref[22:24, :] = strip_prior[2 * plane : 2 * plane + 2, :]

    for l in range(9):
        if l < 2:
            body = low_ref[8 + l].astype(F32)
        elif l < 8:
            body = mask_kz(kz_ref[l - 2], l - 2)
        else:
            body = high_ref[8].astype(F32)
        kzs[l, 0:16, :] = body
        rim(kzs.at[l], 40 + l)
    for l in range(8):
        if l < 1:
            x, y = low_ref[10].astype(F32), low_ref[11].astype(F32)
        elif l < 7:
            x, y = mask_cx(cx_ref[l - 1], 0), mask_cy(cy_ref[l - 1])
        else:
            x, y = high_ref[9].astype(F32), high_ref[10].astype(F32)
        cxs[l, 0:16, :] = x
        cys[l, 0:16, :] = y
        rim(cxs.at[l], 49 + l)
        rim(cys.at[l], 57 + l)
    low_row = low_ref[12].astype(F32) + low_ref[13].astype(F32)
    high_row = high_ref[11].astype(F32) + high_ref[12].astype(F32)
    for l in range(10):
        for c in range(4):
            at = slice(c * 10 + l, c * 10 + l + 1)
            if l < 2:
                decays[at, :] = low_row[c * 2 + l : c * 2 + l + 1]
            elif l < 8:
                decays[at, :] = jnp.full((1, cols), decay_ref[c, l - 2], F32)
            else:
                decays[at, :] = high_row[c * 2 + l - 8 : c * 2 + l - 7]
        if l < 2:
            gains[l : l + 1, :] = low_row[8 + l : 9 + l]
        elif l < 8:
            gains[l : l + 1, :] = jnp.full((1, cols), gain_ref[l - 2], F32)
        else:
            gains[l : l + 1, :] = high_row[l : l + 1]
    for c in range(4):
        total = jnp.zeros((16, cols), F32)
        for l in range(10):
            if l < 2:
                body = low_ref[c * 2 + l].astype(F32)
            elif l < 8:
                body = lam_ref[c, l - 2]
                total = total + profile_ref[c, l - 2] * body
            else:
                body = high_ref[c * 2 + l - 8].astype(F32)
            scaled[l, 0:16, :] = body
            rim(scaled.at[l], c * 10 + l)
            scaled[l] = scaled[l] * decays[c * 10 + l : c * 10 + l + 1, :]
        surface_ref[c] = total

        def both(l):
            at = c * 10 + l
            return decays[at : at + 1, :] * gains[l : l + 1, :]

        for l in range(1, 9):
            here = scaled[l]
            above, below = kzs[l], kzs[l - 1]
            mixed_ref[c, l - 1] = (
                here + above * (scaled[l + 1] - here) - below * (here - scaled[l - 1])
            )
            gain = both(l)
            coef_ref[c, l - 1] = (
                gain + above * (both(l + 1) - gain) - below * (gain - both(l - 1))
            )


def roll(x, shift, axis):
    return pltpu.roll(x, shift % x.shape[axis], axis)


def advect(m, cx, cy, rows):
    gx = roll(m, -1, 0) - m
    back = roll(jnp.minimum(cx, 0.0) * gx, 1, 0)
    value = m[:rows] + jnp.maximum(cx[:rows], 0.0) * gx[:rows] + back[:rows]
    m, cy = m[:rows], cy[:rows]
    gy = roll(m, -1, 1) - m
    return value + jnp.maximum(cy, 0.0) * gy + roll(jnp.minimum(cy, 0.0) * gy, 1, 1)


def first_kernel(
    gain_ref,
    profile_ref,
    cxs,
    cys,
    mixed_ref,
    coef_ref,
    early_ref,
    decays,
    map_ref,
    later_ref,
    surface_ref,
    blocks,
    field,
):
    cols = early_ref.shape[2]
    groups, parts = cols // 128, map_ref.shape[0]
    total = map_ref[0]
    for k in range(1, parts):
        total = total + map_ref[k]
    blocks[0:144, :] = total[0:144]
    blocks[144:176, :] = jnp.zeros((32, 128), F32)
    blocks[176:192, :] = total[144:160]
    for q in range(groups):
        field[:, q * 128 : (q + 1) * 128] = blocks[pl.ds(q, ROWS, stride=groups), :]

    def tracer(c, _):
        weight = 0.0
        for l in range(6):
            weight = weight + profile_ref[c, l] * gain_ref[l]
        total = early_ref[c] + weight * field[0:16, :]
        for l in range(8):
            m = mixed_ref[c, l] + coef_ref[c, l] * field[...]
            value = advect(m, cxs[l], cys[l], ROWS)
            if 1 <= l < 7:
                total = total + profile_ref[c, l - 1] * value[0:16]
            later_ref[c, l] = decays[pl.ds(c * 10 + l + 1, 1), :] * value
        for q in range(groups):
            surface_ref[q, pl.ds(c * 16, 16), :] = total[:, q * 128 : (q + 1) * 128]
        return 0

    lax.fori_loop(0, early_ref.shape[0], tracer, 0)


def second_kernel(kzs, cxs, cys, later_ref, out_ref):
    def tracer(c, _):
        for l in range(6):
            here = later_ref[c, l + 1]
            m = (
                here
                + kzs[l + 2] * (later_ref[c, l + 2] - here)
                - kzs[l + 1] * (here - later_ref[c, l])
            )
            out_ref[c, l] = advect(m, cxs[l + 1], cys[l + 1], 16)
        return 0

    lax.fori_loop(0, out_ref.shape[0], tracer, 0)


def on_device(
    lam_in,
    courant_x,
    courant_y,
    kz_face,
    loss_rate,
    profile,
    kernel,
    obs_values,
    obs_tile,
    obs_block,
):
    size_x, size_core, size_z, size_y = SPLIT
    lev_count, tile_count = size_x * size_core, size_z * size_y
    members = lev_count * size_y
    tracers, levels, rows, cols = lam_in.shape
    blocks = rows * cols // 128
    vmem = pl.BlockSpec(memory_space=pltpu.VMEM)
    smem = pl.BlockSpec(memory_space=pltpu.SMEM)
    anywhere = pl.BlockSpec(memory_space=pl.ANY)
    shape = jax.ShapeDtypeStruct

    def call(body, outs, specs, scratch=(), flops=0, moved=0, limit=VMEM):
        return pl.pallas_call(
            body,
            out_shape=outs,
            in_specs=specs,
            out_specs=jax.tree.map(lambda _: vmem, outs),
            scratch_shapes=[pltpu.VMEM(s, F32) if isinstance(s, tuple) else s for s in scratch],
            compiler_params=pltpu.CompilerParams(vmem_limit_bytes=limit),
            cost_estimate=pl.CostEstimate(flops=flops, bytes_accessed=moved, transcendentals=0),
        )

    where = jnp.stack(
        [
            (lax.axis_index(TILE) == tile_count - 1).astype(jnp.int32),
            (lax.axis_index(LEV) == lev_count - 1).astype(jnp.int32),
        ]
    )
    decay = jnp.exp(-loss_rate)

    packed = call(
        pack_kernel,
        shape((members, 2 * CAP + 16, 128), BF16),
        [anywhere] * 3,
        scratch=[
            pltpu.VMEM((1, obs_values.shape[0]), jnp.int32),
            pltpu.VMEM((1, obs_values.shape[0]), jnp.int32),
            pltpu.VMEM(obs_values.shape, BF16),
            (obs_values.shape[0] + 2 * CAP, 128),
            pltpu.VMEM((8, 128), jnp.int32),
            pltpu.SMEM((8, 128), jnp.int32),
            pltpu.SemaphoreType.DMA((4,)),
        ],
        flops=1 << 30,
        moved=2 << 20,
        limit=MOST,
    )(obs_tile.reshape(1, -1), obs_block.reshape(1, -1), obs_values)
    got = lax.all_to_all(packed, LEV + ("y",), 0, 0, tiled=True)

    up, down = call(
        level_kernel,
        (shape((14, rows, cols), BF16), shape((13, rows, cols), BF16)),
        [smem] * 3 + [vmem] * 4 + [anywhere],
        moved=4 << 20,
    )(where, decay, kernel, lam_in, kz_face, courant_x, courant_y, packed)
    low = chain(LEV, lev_count, 1)(up)
    high = chain(LEV, lev_count, -1)(down)
    first_rows, last_rows = call(
        row_kernel,
        (shape((STRIP, cols), BF16), shape((STRIP, cols), BF16)),
        [smem] + [vmem] * 6,
        scratch=[(STRIP, cols)],
        moved=5 << 20,
    )(where, lam_in, kz_face, courant_x, courant_y, low, high)
    after = chain(TILE, tile_count, -1)(first_rows)
    prior = chain(TILE, tile_count, 1)(last_rows)
    kzs, cxs, cys, mixed, coef, early, decays = call(
        ready_kernel,
        (
            shape((9, ROWS, cols), F32),
            shape((8, ROWS, cols), F32),
            shape((8, ROWS, cols), F32),
            shape((tracers, 8, ROWS, cols), F32),
            shape((tracers, 8, ROWS, cols), F32),
            shape((tracers, rows, cols), F32),
            shape((10 * tracers, cols), F32),
        ),
        [smem] * 4 + [vmem] * 8,
        scratch=[(STRIP, cols), (STRIP, cols), (16, cols), (10, ROWS, cols)],
        moved=12 << 20,
    )(
        where,
        decay,
        kernel,
        profile,
        lam_in,
        kz_face,
        courant_x,
        courant_y,
        low,
        high,
        after,
        prior,
    )

    sums = call(
        sum_kernel, shape((2, blocks, 128), F32), [vmem], flops=1 << 28, moved=1 << 20
    )(got)

    def along_z(value, j):
        perm = [
            (k * size_z + z, k * size_z + (z + SHIFTS[k][j]) % size_z)
            for k in range(lev_count)
            for z in range(size_z)
        ]
        return lax.ppermute(value, LEV + ("z",), perm)

    part = along_z(sums[0], 0) + along_z(sums[1], 1)
    edge = 2 * cols // 128
    part_after = chain(TILE, tile_count, -1)(part[:edge])
    part_prior = chain(TILE, tile_count, 1)(part[-edge:])
    parts = lax.all_gather(jnp.concatenate([part, part_after, part_prior]), LEV, axis=0)

    later, surface = call(
        first_kernel,
        (
            shape((tracers, 8, ROWS, cols), F32),
            shape((lev_count, tracers * rows, cols // lev_count), F32),
        ),
        [smem] * 2 + [vmem] * 7,
        scratch=[(ROWS * cols // 128, 128), (ROWS, cols)],
        moved=8 << 20,
    )(kernel, profile, cxs, cys, mixed, coef, early, decays, parts)
    shares = lax.all_to_all(surface, LEV, 0, 0, tiled=True)
    lam_out = call(
        second_kernel, shape(lam_in.shape, F32), [vmem] * 4, moved=6 << 20
    )(kzs, cxs, cys, later)
    gradient = jnp.sum(shares, axis=0).reshape(tracers, rows, cols // lev_count)
    return lam_out, gradient


def solution(mesh):
    grid = Mesh(np.asarray(mesh.devices).reshape(SPLIT), ("x", "core", "z", "y"))
    in_specs = (
        P(None, LEV, TILE, None),
        P(LEV, TILE, None),
        P(LEV, TILE, None),
        P(LEV, TILE, None),
        P(None, LEV),
        P(None, LEV),
        P(LEV),
        P(LEV + TILE, None),
        P(LEV + TILE, None),
        P(LEV + TILE),
    )
    out_specs = (P(None, LEV, TILE, None), P(None, TILE, LEV))
    return jax.shard_map(
        on_device, mesh=grid, in_specs=in_specs, out_specs=out_specs, check_vma=False
    )
```

```python
import functools

import jax
import jax.numpy as jnp
import numpy as np
from jax import lax
from jax.experimental import pallas as pl
from jax.experimental.pallas import tpu as pltpu
from jax.sharding import Mesh
from jax.sharding import PartitionSpec as P

SPLIT = (4, 2, 16, 4)
SHIFTS = ((0, 8), (1, 15), (2, 14), (7, 9), (3, 13), (6, 10), (4, 12), (5, 11))
CAP = 64
LEV = ("x", "core")
TILE = ("z", "y")
ROWS = 24
STRIP = 144
VMEM = 24 * 1024 * 1024
MOST = 63487488
F32, BF16 = jnp.float32, jnp.bfloat16


def chain(axes, count, steps):
    first, last = max(0, -steps), min(count, count - steps)
    return functools.partial(
        lax.ppermute, axis_name=axes, perm=[(i, i + steps) for i in range(first, last)]
    )


def iota(shape, dim):
    return lax.broadcasted_iota(jnp.int32, shape, dim)


def rank_of(tile, here, size_z, size_y):
    distance = tile // size_y - here
    distance = jnp.where(distance < 0, distance + size_z, distance)
    order = 2 * (tile % size_y)
    for k, both in enumerate(SHIFTS):
        for j, d in enumerate(both):
            order = order + jnp.where(distance == d, 2 * size_y * k + j, 0)
    return order


def one(mask):
    return mask.astype(F32).astype(BF16)


def pack_kernel(
    tile_hbm,
    block_hbm,
    obs_hbm,
    out_ref,
    tile_ref,
    block_ref,
    obs_ref,
    ordered,
    starts,
    starts_smem,
    sems,
):
    size_z, size_y = SPLIT[2:]
    tiles = size_z * size_y
    members, depth, _ = out_ref.shape
    count = obs_ref.shape[0]
    pair, part = 2 * CAP, 256
    copies = [
        pltpu.make_async_copy(tile_hbm, tile_ref, sems.at[0]),
        pltpu.make_async_copy(block_hbm, block_ref, sems.at[1]),
        pltpu.make_async_copy(obs_hbm, obs_ref, sems.at[2]),
    ]
    for copy in copies:
        copy.start()
    here = lax.axis_index("z")
    order = rank_of(iota((tiles, 1), 0), here, size_z, size_y)
    order_row = rank_of(iota((1, tiles), 1), here, size_z, size_y)
    before = (iota((part, part), 0) < iota((part, part), 1)).astype(BF16)
    copies[0].wait()
    hot = (iota((tiles, count), 0) == tile_ref[...]).astype(F32)
    cuts = [hot[:, i : i + part] for i in range(0, count, part)]
    counts = [jnp.sum(cut, axis=1, keepdims=True) for cut in cuts]
    amount = counts[0]
    for more in counts[1:]:
        amount = amount + more
    amounts = jnp.broadcast_to(amount, (tiles, 128)).astype(BF16)
    first = jnp.dot(one(order_row < order), amounts, preferred_element_type=F32)[:, :1]
    opening = jnp.dot(one(order_row // 2 < order // 2), amounts, preferred_element_type=F32)[:, :1]
    ahead = jnp.where(order < 2 * iota((tiles, 128), 1), amount, 0.0)
    ahead = jnp.sum(ahead, axis=0, keepdims=True)
    starts[...] = jnp.broadcast_to(ahead, (8, 128)).astype(jnp.int32)
    sent = pltpu.make_async_copy(starts, starts_smem, sems.at[3])
    sent.start()
    rank = jnp.dot(
        jnp.concatenate(cuts, axis=0).astype(BF16), before, preferred_element_type=F32
    )
    tag = (pair * order).astype(F32)
    places, slots = [], []
    for i, cut in enumerate(cuts):
        at = rank[i * tiles : (i + 1) * tiles] + first
        places.append(jnp.sum(cut * at, axis=0, keepdims=True))
        slots.append(jnp.sum(cut * (at - opening + tag), axis=0, keepdims=True))
        first = first + counts[i]
    place = jnp.concatenate(places, axis=1).astype(jnp.int32)
    slot = jnp.concatenate(slots, axis=1).astype(jnp.int32)
    tile_order = slot // pair
    slot = slot - tile_order * pair
    copies[1].wait()
    code = (block_ref[...] + 1 + 128 * (tile_order % 2)).astype(F32)
    codes = lax.dot_general(
        one(iota((members, count), 0) == tile_order // 2),
        jnp.where(iota((pair, count), 0) == slot, code, 0.0).astype(BF16),
        (((1,), (1,)), ((), ())),
        preferred_element_type=F32,
    ).astype(BF16)
    out_ref[:, pair:, :] = jnp.broadcast_to(codes[:, None, :], (members, depth - pair, 128))
    copies[2].wait()
    for i in range(0, count, part):
        pick = one(iota((part, count), 0) + i == place)
        ordered[i : i + part, :] = jnp.dot(pick, obs_ref[...], preferred_element_type=F32)
    ordered[count : count + pair, :] = jnp.zeros((pair, 128), F32)
    sent.wait()
    for m in range(members):
        rows = ordered[pl.ds(starts_smem[0, m], pair), :]
        out_ref[m, :pair, :] = rows.astype(BF16)


def sum_kernel(got_ref, out_ref):
    sources = got_ref.shape[0]
    pair = 2 * CAP
    total = jnp.zeros((256, 128), F32)
    for s in range(0, sources, 2):
        code = jnp.concatenate(
            [got_ref[s + i, pair : pair + 16, :].astype(F32)[:1] for i in range(2)], axis=1
        )
        pick = iota((256, 2 * pair), 0) + 1 == code.astype(jnp.int32)
        rows = jnp.concatenate([got_ref[s + i, :pair, :] for i in range(2)], axis=0)
        total += jnp.dot(pick.astype(BF16), rows, preferred_element_type=F32)
    out_ref[...] = total.reshape(2, 128, 128)


def masks(where_ref):
    def kz(value, level):
        return jnp.where(where_ref[1] == 1, 0.0, value) if level == 5 else value

    def cx(value, first):
        last = iota(value.shape, 0) + first == 15
        return jnp.where(last & (where_ref[0] == 1), 0.0, value)

    def cy(value):
        return jnp.where(iota(value.shape, 1) == value.shape[1] - 1, 0.0, value)

    return kz, cx, cy


def level_kernel(
    where_ref, decay_ref, gain_ref, lam_ref, kz_ref, cx_ref, cy_ref, after_ref, up_ref, down_ref
):
    mask_kz, mask_cx, mask_cy = masks(where_ref)
    for ref, first in ((up_ref, 4), (down_ref, 0)):
        for c in range(4):
            for i in range(2):
                ref[c * 2 + i] = lam_ref[c, first + i].astype(BF16)
        levels = (4, 5) if first else (0,)
        for i, level in enumerate(levels):
            ref[8 + i] = mask_kz(kz_ref[level], level).astype(BF16)
        at = 8 + len(levels)
        ref[at] = mask_cx(cx_ref[levels[-1]], 0).astype(BF16)
        ref[at + 1] = mask_cy(cy_ref[levels[-1]]).astype(BF16)
        row = iota(ref.shape[1:], 0)
        plane = jnp.zeros(ref.shape[1:], F32)
        for i in range(2):
            plane = jnp.where(row == 8 + i, gain_ref[first + i], plane)
            for c in range(4):
                plane = jnp.where(row == c * 2 + i, decay_ref[c, first + i], plane)
        rough = plane.astype(BF16)
        ref[at + 2] = rough
        ref[at + 3] = (plane - rough.astype(F32)).astype(BF16)


def row_kernel(
    where_ref, lam_ref, kz_ref, cx_ref, cy_ref, low_ref, high_ref, prior_ref, next_ref, strip
):
    mask_kz, mask_cx, mask_cy = masks(where_ref)
    for ref, first in ((prior_ref, 0), (next_ref, 14)):
        rows = slice(first, first + 2)

        def put(plane, value):
            strip[2 * plane : 2 * plane + 2, :] = value

        strip[130:144, :] = jnp.zeros((14, strip.shape[1]), F32)
        for c in range(4):
            for l in range(10):
                if l < 2:
                    value = low_ref[c * 2 + l].astype(F32)[rows]
                elif l < 8:
                    value = lam_ref[c, l - 2, rows, :]
                else:
                    value = high_ref[c * 2 + l - 8].astype(F32)[rows]
                put(c * 10 + l, value)
        for l in range(9):
            if l < 2:
                value = low_ref[8 + l].astype(F32)[rows]
            elif l < 8:
                value = mask_kz(kz_ref[l - 2, rows, :], l - 2)
            else:
                value = high_ref[8].astype(F32)[rows]
            put(40 + l, value)
        for l in range(8):
            if l < 1:
                x, y = low_ref[10].astype(F32)[rows], low_ref[11].astype(F32)[rows]
            elif l < 7:
                x = mask_cx(cx_ref[l - 1, rows, :], first)
                y = mask_cy(cy_ref[l - 1, rows, :])
            else:
                x, y = high_ref[9].astype(F32)[rows], high_ref[10].astype(F32)[rows]
            put(49 + l, x)
            put(57 + l, y)
        ref[...] = strip[...].astype(BF16)


def ready_kernel(
    where_ref,
    decay_ref,
    gain_ref,
    profile_ref,
    lam_ref,
    kz_ref,
    cx_ref,
    cy_ref,
    low_ref,
    high_ref,
    after_ref,
    prior_ref,
    kzs,
    cxs,
    cys,
    mixed_ref,
    coef_ref,
    surface_ref,
    decays,
    strip_after,
    strip_prior,
    gains,
    scaled,
):
    mask_kz, mask_cx, mask_cy = masks(where_ref)
    cols = lam_ref.shape[3]
    strip_after[...] = after_ref[...].astype(F32)
    strip_prior[...] = prior_ref[...].astype(F32)

    def rim(ref, plane):
        if ref.shape[0] == ROWS:
            ref[16:24, :] = jnp.zeros((8, cols), F32)
            ref[16:18, :] = strip_after[2 * plane : 2 * plane + 2, :]
            ref[22:24, :] = strip_prior[2 * plane : 2 * plane + 2, :]

    for l in range(9):
        if l < 2:
            body = low_ref[8 + l].astype(F32)
        elif l < 8:
            body = mask_kz(kz_ref[l - 2], l - 2)
        else:
            body = high_ref[8].astype(F32)
        kzs[l, 0:16, :] = body
        rim(kzs.at[l], 40 + l)
    for l in range(8):
        if l < 1:
            x, y = low_ref[10].astype(F32), low_ref[11].astype(F32)
        elif l < 7:
            x, y = mask_cx(cx_ref[l - 1], 0), mask_cy(cy_ref[l - 1])
        else:
            x, y = high_ref[9].astype(F32), high_ref[10].astype(F32)
        cxs[l, 0:16, :] = x
        cys[l, 0:16, :] = y
        rim(cxs.at[l], 49 + l)
        rim(cys.at[l], 57 + l)
    low_row = low_ref[12].astype(F32) + low_ref[13].astype(F32)
    high_row = high_ref[11].astype(F32) + high_ref[12].astype(F32)
    for l in range(10):
        for c in range(4):
            at = slice(c * 10 + l, c * 10 + l + 1)
            if l < 2:
                decays[at, :] = low_row[c * 2 + l : c * 2 + l + 1]
            elif l < 8:
                decays[at, :] = jnp.full((1, cols), decay_ref[c, l - 2], F32)
            else:
                decays[at, :] = high_row[c * 2 + l - 8 : c * 2 + l - 7]
        if l < 2:
            gains[l : l + 1, :] = low_row[8 + l : 9 + l]
        elif l < 8:
            gains[l : l + 1, :] = jnp.full((1, cols), gain_ref[l - 2], F32)
        else:
            gains[l : l + 1, :] = high_row[l : l + 1]
    for c in range(4):
        total = jnp.zeros((16, cols), F32)
        for l in range(10):
            if l < 2:
                body = low_ref[c * 2 + l].astype(F32)
            elif l < 8:
                body = lam_ref[c, l - 2]
                total = total + profile_ref[c, l - 2] * body
            else:
                body = high_ref[c * 2 + l - 8].astype(F32)
            scaled[l, 0:16, :] = body
            rim(scaled.at[l], c * 10 + l)
            scaled[l] = scaled[l] * decays[c * 10 + l : c * 10 + l + 1, :]
        surface_ref[c] = total

        def both(l):
            at = c * 10 + l
            return decays[at : at + 1, :] * gains[l : l + 1, :]

        for l in range(1, 9):
            here = scaled[l]
            above, below = kzs[l], kzs[l - 1]
            mixed_ref[c, l - 1] = (
                here + above * (scaled[l + 1] - here) - below * (here - scaled[l - 1])
            )
            gain = both(l)
            coef_ref[c, l - 1] = (
                gain + above * (both(l + 1) - gain) - below * (gain - both(l - 1))
            )


def roll(x, shift, axis):
    return pltpu.roll(x, shift % x.shape[axis], axis)


def advect(m, cx, cy, rows):
    gx = roll(m, -1, 0) - m
    back = roll(jnp.minimum(cx, 0.0) * gx, 1, 0)
    value = m[:rows] + jnp.maximum(cx[:rows], 0.0) * gx[:rows] + back[:rows]
    m, cy = m[:rows], cy[:rows]
    gy = roll(m, -1, 1) - m
    return value + jnp.maximum(cy, 0.0) * gy + roll(jnp.minimum(cy, 0.0) * gy, 1, 1)


def first_kernel(
    gain_ref,
    profile_ref,
    cxs,
    cys,
    mixed_ref,
    coef_ref,
    early_ref,
    decays,
    map_ref,
    later_ref,
    surface_ref,
    blocks,
    field,
):
    cols = early_ref.shape[2]
    groups, parts = cols // 128, map_ref.shape[0]
    total = map_ref[0]
    for k in range(1, parts):
        total = total + map_ref[k]
    blocks[0:144, :] = total[0:144]
    blocks[144:176, :] = jnp.zeros((32, 128), F32)
    blocks[176:192, :] = total[144:160]
    for q in range(groups):
        field[:, q * 128 : (q + 1) * 128] = blocks[pl.ds(q, ROWS, stride=groups), :]

    def tracer(c, _):
        weight = 0.0
        for l in range(6):
            weight = weight + profile_ref[c, l] * gain_ref[l]
        total = early_ref[c] + weight * field[0:16, :]
        for l in range(8):
            m = mixed_ref[c, l] + coef_ref[c, l] * field[...]
            value = advect(m, cxs[l], cys[l], ROWS)
            if 1 <= l < 7:
                total = total + profile_ref[c, l - 1] * value[0:16]
            later_ref[c, l] = decays[pl.ds(c * 10 + l + 1, 1), :] * value
        for q in range(groups):
            surface_ref[q, pl.ds(c * 16, 16), :] = total[:, q * 128 : (q + 1) * 128]
        return 0

    lax.fori_loop(0, early_ref.shape[0], tracer, 0)


def second_kernel(kzs, cxs, cys, later_ref, out_ref):
    def tracer(c, _):
        for l in range(6):
            here = later_ref[c, l + 1]
            m = (
                here
                + kzs[l + 2] * (later_ref[c, l + 2] - here)
                - kzs[l + 1] * (here - later_ref[c, l])
            )
            out_ref[c, l] = advect(m, cxs[l + 1], cys[l + 1], 16)
        return 0

    lax.fori_loop(0, out_ref.shape[0], tracer, 0)


def on_device(
    lam_in,
    courant_x,
    courant_y,
    kz_face,
    loss_rate,
    profile,
    kernel,
    obs_values,
    obs_tile,
    obs_block,
):
    size_x, size_core, size_z, size_y = SPLIT
    lev_count, tile_count = size_x * size_core, size_z * size_y
    members = lev_count * size_y
    tracers, levels, rows, cols = lam_in.shape
    blocks = rows * cols // 128
    vmem = pl.BlockSpec(memory_space=pltpu.VMEM)
    smem = pl.BlockSpec(memory_space=pltpu.SMEM)
    anywhere = pl.BlockSpec(memory_space=pl.ANY)
    shape = jax.ShapeDtypeStruct

    def call(body, outs, specs, scratch=(), flops=0, moved=0, limit=VMEM):
        return pl.pallas_call(
            body,
            out_shape=outs,
            in_specs=specs,
            out_specs=jax.tree.map(lambda _: vmem, outs),
            scratch_shapes=[pltpu.VMEM(s, F32) if isinstance(s, tuple) else s for s in scratch],
            compiler_params=pltpu.CompilerParams(vmem_limit_bytes=limit),
            cost_estimate=pl.CostEstimate(flops=flops, bytes_accessed=moved, transcendentals=0),
        )

    where = jnp.stack(
        [
            (lax.axis_index(TILE) == tile_count - 1).astype(jnp.int32),
            (lax.axis_index(LEV) == lev_count - 1).astype(jnp.int32),
        ]
    )
    decay = jnp.exp(-loss_rate)

    packed = call(
        pack_kernel,
        shape((members, 2 * CAP + 16, 128), BF16),
        [anywhere] * 3,
        scratch=[
            pltpu.VMEM((1, obs_values.shape[0]), jnp.int32),
            pltpu.VMEM((1, obs_values.shape[0]), jnp.int32),
            pltpu.VMEM(obs_values.shape, BF16),
            (obs_values.shape[0] + 2 * CAP, 128),
            pltpu.VMEM((8, 128), jnp.int32),
            pltpu.SMEM((8, 128), jnp.int32),
            pltpu.SemaphoreType.DMA((4,)),
        ],
        flops=1 << 30,
        moved=2 << 20,
        limit=MOST,
    )(obs_tile.reshape(1, -1), obs_block.reshape(1, -1), obs_values)
    got = lax.all_to_all(packed, LEV + ("y",), 0, 0, tiled=True)

    up, down = call(
        level_kernel,
        (shape((14, rows, cols), BF16), shape((13, rows, cols), BF16)),
        [smem] * 3 + [vmem] * 4 + [anywhere],
        moved=4 << 20,
        limit=MOST,
    )(where, decay, kernel, lam_in, kz_face, courant_x, courant_y, packed)
    low = chain(LEV, lev_count, 1)(up)
    high = chain(LEV, lev_count, -1)(down)
    first_rows, last_rows = call(
        row_kernel,
        (shape((STRIP, cols), BF16), shape((STRIP, cols), BF16)),
        [smem] + [vmem] * 6,
        scratch=[(STRIP, cols)],
        moved=5 << 20,
    )(where, lam_in, kz_face, courant_x, courant_y, low, high)
    after = chain(TILE, tile_count, -1)(first_rows)
    prior = chain(TILE, tile_count, 1)(last_rows)
    kzs, cxs, cys, mixed, coef, early, decays = call(
        ready_kernel,
        (
            shape((9, ROWS, cols), F32),
            shape((8, ROWS, cols), F32),
            shape((8, ROWS, cols), F32),
            shape((tracers, 8, ROWS, cols), F32),
            shape((tracers, 8, ROWS, cols), F32),
            shape((tracers, rows, cols), F32),
            shape((10 * tracers, cols), F32),
        ),
        [smem] * 4 + [vmem] * 8,
        scratch=[(STRIP, cols), (STRIP, cols), (16, cols), (10, ROWS, cols)],
        moved=12 << 20,
    )(
        where,
        decay,
        kernel,
        profile,
        lam_in,
        kz_face,
        courant_x,
        courant_y,
        low,
        high,
        after,
        prior,
    )

    sums = call(
        sum_kernel, shape((2, blocks, 128), F32), [vmem], flops=1 << 28, moved=1 << 20
    )(got)

    def along_z(value, j):
        perm = [
            (k * size_z + z, k * size_z + (z + SHIFTS[k][j]) % size_z)
            for k in range(lev_count)
            for z in range(size_z)
        ]
        return lax.ppermute(value, LEV + ("z",), perm)

    part = along_z(sums[0], 0) + along_z(sums[1], 1)
    edge = 2 * cols // 128
    part_after = chain(TILE, tile_count, -1)(part[:edge])
    part_prior = chain(TILE, tile_count, 1)(part[-edge:])
    parts = lax.all_gather(jnp.concatenate([part, part_after, part_prior]), LEV, axis=0)

    later, surface = call(
        first_kernel,
        (
            shape((tracers, 8, ROWS, cols), F32),
            shape((lev_count, tracers * rows, cols // lev_count), F32),
        ),
        [smem] * 2 + [vmem] * 7,
        scratch=[(ROWS * cols // 128, 128), (ROWS, cols)],
        moved=8 << 20,
    )(kernel, profile, cxs, cys, mixed, coef, early, decays, parts)
    shares = lax.all_to_all(surface, LEV, 0, 0, tiled=True)
    lam_out = call(
        second_kernel, shape(lam_in.shape, F32), [vmem] * 4, moved=6 << 20
    )(kzs, cxs, cys, later)
    gradient = jnp.sum(shares, axis=0).reshape(tracers, rows, cols // lev_count)
    return lam_out, gradient


def solution(mesh):
    grid = Mesh(np.asarray(mesh.devices).reshape(SPLIT), ("x", "core", "z", "y"))
    in_specs = (
        P(None, LEV, TILE, None),
        P(LEV, TILE, None),
        P(LEV, TILE, None),
        P(LEV, TILE, None),
        P(None, LEV),
        P(None, LEV),
        P(LEV),
        P(LEV + TILE, None),
        P(LEV + TILE, None),
        P(LEV + TILE),
    )
    out_specs = (P(None, LEV, TILE, None), P(None, TILE, LEV))
    return jax.shard_map(
        on_device, mesh=grid, in_specs=in_specs, out_specs=out_specs, check_vma=False
    )
```

```python
import functools

import jax
import jax.numpy as jnp
import numpy as np
from jax import lax
from jax.experimental import pallas as pl
from jax.experimental.pallas import tpu as pltpu
from jax.sharding import Mesh
from jax.sharding import PartitionSpec as P

SPLIT = (4, 2, 16, 4)
SHIFTS = ((0, 8), (1, 15), (2, 14), (7, 9), (3, 13), (6, 10), (4, 12), (5, 11))
CAP = 64
LEV = ("x", "core")
TILE = ("z", "y")
ROWS = 24
STRIP = 144
OWN = 96
VMEM = 24 * 1024 * 1024
MOST = 63487488
F32, BF16 = jnp.float32, jnp.bfloat16


def chain(axes, count, steps):
    first, last = max(0, -steps), min(count, count - steps)
    return functools.partial(
        lax.ppermute, axis_name=axes, perm=[(i, i + steps) for i in range(first, last)]
    )


def iota(shape, dim):
    return lax.broadcasted_iota(jnp.int32, shape, dim)


def rank_of(tile, here, size_z, size_y):
    distance = tile // size_y - here
    distance = jnp.where(distance < 0, distance + size_z, distance)
    order = 2 * (tile % size_y)
    for k, both in enumerate(SHIFTS):
        for j, d in enumerate(both):
            order = order + jnp.where(distance == d, 2 * size_y * k + j, 0)
    return order


def one(mask):
    return mask.astype(F32).astype(BF16)


def pack_kernel(
    tile_hbm,
    block_hbm,
    obs_hbm,
    out_ref,
    tile_ref,
    block_ref,
    obs_ref,
    ordered,
    starts,
    starts_smem,
    sems,
):
    size_z, size_y = SPLIT[2:]
    tiles = size_z * size_y
    members, depth, _ = out_ref.shape
    count = obs_ref.shape[0]
    pair, part = 2 * CAP, 256
    copies = [
        pltpu.make_async_copy(tile_hbm, tile_ref, sems.at[0]),
        pltpu.make_async_copy(block_hbm, block_ref, sems.at[1]),
        pltpu.make_async_copy(obs_hbm, obs_ref, sems.at[2]),
    ]
    for copy in copies:
        copy.start()
    here = lax.axis_index("z")
    order = rank_of(iota((tiles, 1), 0), here, size_z, size_y)
    order_row = rank_of(iota((1, tiles), 1), here, size_z, size_y)
    before = (iota((part, part), 0) < iota((part, part), 1)).astype(BF16)
    copies[0].wait()
    hot = (iota((tiles, count), 0) == tile_ref[...]).astype(F32)
    cuts = [hot[:, i : i + part] for i in range(0, count, part)]
    counts = [jnp.sum(cut, axis=1, keepdims=True) for cut in cuts]
    amount = counts[0]
    for more in counts[1:]:
        amount = amount + more
    amounts = jnp.broadcast_to(amount, (tiles, 128)).astype(BF16)
    first = jnp.dot(one(order_row < order), amounts, preferred_element_type=F32)[:, :1]
    opening = jnp.dot(one(order_row // 2 < order // 2), amounts, preferred_element_type=F32)[:, :1]
    ahead = jnp.where(order < 2 * iota((tiles, 128), 1), amount, 0.0)
    ahead = jnp.sum(ahead, axis=0, keepdims=True)
    starts[...] = jnp.broadcast_to(ahead, (8, 128)).astype(jnp.int32)
    sent = pltpu.make_async_copy(starts, starts_smem, sems.at[3])
    sent.start()
    rank = jnp.dot(
        jnp.concatenate(cuts, axis=0).astype(BF16), before, preferred_element_type=F32
    )
    tag = (pair * order).astype(F32)
    places, slots = [], []
    for i, cut in enumerate(cuts):
        at = rank[i * tiles : (i + 1) * tiles] + first
        places.append(jnp.sum(cut * at, axis=0, keepdims=True))
        slots.append(jnp.sum(cut * (at - opening + tag), axis=0, keepdims=True))
        first = first + counts[i]
    place = jnp.concatenate(places, axis=1).astype(jnp.int32)
    slot = jnp.concatenate(slots, axis=1).astype(jnp.int32)
    tile_order = slot // pair
    slot = slot - tile_order * pair
    copies[1].wait()
    code = (block_ref[...] + 1 + 128 * (tile_order % 2)).astype(F32)
    codes = lax.dot_general(
        one(iota((members, count), 0) == tile_order // 2),
        jnp.where(iota((pair, count), 0) == slot, code, 0.0).astype(BF16),
        (((1,), (1,)), ((), ())),
        preferred_element_type=F32,
    ).astype(BF16)
    out_ref[:, pair:, :] = jnp.broadcast_to(codes[:, None, :], (members, depth - pair, 128))
    copies[2].wait()
    for i in range(0, count, part):
        pick = one(iota((part, count), 0) + i == place)
        ordered[i : i + part, :] = jnp.dot(pick, obs_ref[...], preferred_element_type=F32)
    ordered[count : count + pair, :] = jnp.zeros((pair, 128), F32)
    sent.wait()
    for m in range(members):
        rows = ordered[pl.ds(starts_smem[0, m], pair), :]
        out_ref[m, :pair, :] = rows.astype(BF16)


def sum_kernel(got_ref, out_ref):
    sources = got_ref.shape[0]
    pair = 2 * CAP
    total = jnp.zeros((256, 128), F32)
    for s in range(0, sources, 2):
        code = jnp.concatenate(
            [got_ref[s + i, pair : pair + 16, :].astype(F32)[:1] for i in range(2)], axis=1
        )
        pick = iota((256, 2 * pair), 0) + 1 == code.astype(jnp.int32)
        rows = jnp.concatenate([got_ref[s + i, :pair, :] for i in range(2)], axis=0)
        total += jnp.dot(pick.astype(BF16), rows, preferred_element_type=F32)
    out_ref[...] = total.reshape(2, 128, 128)


def masks(where_ref):
    def kz(value, level):
        return jnp.where(where_ref[1] == 1, 0.0, value) if level == 5 else value

    def cx(value, first):
        last = iota(value.shape, 0) + first == 15
        return jnp.where(last & (where_ref[0] == 1), 0.0, value)

    def cy(value):
        return jnp.where(iota(value.shape, 1) == value.shape[1] - 1, 0.0, value)

    return kz, cx, cy


def level_kernel(
    where_ref, decay_ref, gain_ref, lam_ref, kz_ref, cx_ref, cy_ref, after_ref, up_ref, down_ref, prior_ref, next_ref, strip
):
    mask_kz, mask_cx, mask_cy = masks(where_ref)
    for ref, first in ((prior_ref, 0), (next_ref, 14)):
        rows = slice(first, first + 2)

        def put(plane, value):
            strip[2 * plane : 2 * plane + 2, :] = value

        strip[84:OWN, :] = jnp.zeros((OWN - 84, strip.shape[1]), F32)
        for l in range(6):
            for c in range(4):
                put(c * 6 + l, lam_ref[c, l, rows, :])
            put(24 + l, mask_kz(kz_ref[l, rows, :], l))
            put(30 + l, mask_cx(cx_ref[l, rows, :], first))
            put(36 + l, mask_cy(cy_ref[l, rows, :]))
        ref[...] = strip[...].astype(BF16)
    for ref, first in ((up_ref, 4), (down_ref, 0)):
        for c in range(4):
            for i in range(2):
                ref[c * 2 + i] = lam_ref[c, first + i].astype(BF16)
        levels = (4, 5) if first else (0,)
        for i, level in enumerate(levels):
            ref[8 + i] = mask_kz(kz_ref[level], level).astype(BF16)
        at = 8 + len(levels)
        ref[at] = mask_cx(cx_ref[levels[-1]], 0).astype(BF16)
        ref[at + 1] = mask_cy(cy_ref[levels[-1]]).astype(BF16)
        row = iota(ref.shape[1:], 0)
        plane = jnp.zeros(ref.shape[1:], F32)
        for i in range(2):
            plane = jnp.where(row == 8 + i, gain_ref[first + i], plane)
            for c in range(4):
                plane = jnp.where(row == c * 2 + i, decay_ref[c, first + i], plane)
        rough = plane.astype(BF16)
        ref[at + 2] = rough
        ref[at + 3] = (plane - rough.astype(F32)).astype(BF16)


def row_kernel(own_prior, own_next, low_ref, high_ref, prior_ref, next_ref, strip):
    sources = [(low_ref, i) for i in range(8)] + [(high_ref, i) for i in range(8)]
    sources += [(low_ref, 8), (low_ref, 9), (high_ref, 8), (low_ref, 10), (high_ref, 9)]
    sources += [(low_ref, 11), (high_ref, 10)]
    for ref, own, first in ((prior_ref, own_prior, 0), (next_ref, own_next, 14)):
        ref[0:OWN, :] = own[...]
        for i, (source, plane) in enumerate(sources):
            strip[2 * i : 2 * i + 2, :] = source[plane].astype(F32)[first : first + 2]
        strip[46:48, :] = jnp.zeros((2, strip.shape[1]), F32)
        ref[OWN:STRIP, :] = strip[...].astype(BF16)


def ready_kernel(
    where_ref,
    decay_ref,
    gain_ref,
    profile_ref,
    lam_ref,
    kz_ref,
    cx_ref,
    cy_ref,
    low_ref,
    high_ref,
    after_ref,
    prior_ref,
    kzs,
    cxs,
    cys,
    mixed_ref,
    coef_ref,
    surface_ref,
    decays,
    strip_after,
    strip_prior,
    gains,
    scaled,
):
    mask_kz, mask_cx, mask_cy = masks(where_ref)
    cols = lam_ref.shape[3]
    strip_after[...] = after_ref[...].astype(F32)
    strip_prior[...] = prior_ref[...].astype(F32)

    def rim(ref, plane):
        if ref.shape[0] == ROWS:
            ref[16:24, :] = jnp.zeros((8, cols), F32)
            ref[16:18, :] = strip_after[2 * plane : 2 * plane + 2, :]
            ref[22:24, :] = strip_prior[2 * plane : 2 * plane + 2, :]

    for l in range(9):
        if l < 2:
            body = low_ref[8 + l].astype(F32)
        elif l < 8:
            body = mask_kz(kz_ref[l - 2], l - 2)
        else:
            body = high_ref[8].astype(F32)
        kzs[l, 0:16, :] = body
        rim(kzs.at[l], 64 + l if l < 2 else (22 + l if l < 8 else 66))
    for l in range(8):
        if l < 1:
            x, y = low_ref[10].astype(F32), low_ref[11].astype(F32)
        elif l < 7:
            x, y = mask_cx(cx_ref[l - 1], 0), mask_cy(cy_ref[l - 1])
        else:
            x, y = high_ref[9].astype(F32), high_ref[10].astype(F32)
        cxs[l, 0:16, :] = x
        cys[l, 0:16, :] = y
        rim(cxs.at[l], 67 if l < 1 else (29 + l if l < 7 else 68))
        rim(cys.at[l], 69 if l < 1 else (35 + l if l < 7 else 70))
    low_row = low_ref[12].astype(F32) + low_ref[13].astype(F32)
    high_row = high_ref[11].astype(F32) + high_ref[12].astype(F32)
    for l in range(10):
        for c in range(4):
            at = slice(c * 10 + l, c * 10 + l + 1)
            if l < 2:
                decays[at, :] = low_row[c * 2 + l : c * 2 + l + 1]
            elif l < 8:
                decays[at, :] = jnp.full((1, cols), decay_ref[c, l - 2], F32)
            else:
                decays[at, :] = high_row[c * 2 + l - 8 : c * 2 + l - 7]
        if l < 2:
            gains[l : l + 1, :] = low_row[8 + l : 9 + l]
        elif l < 8:
            gains[l : l + 1, :] = jnp.full((1, cols), gain_ref[l - 2], F32)
        else:
            gains[l : l + 1, :] = high_row[l : l + 1]
    for c in range(4):
        total = jnp.zeros((16, cols), F32)
        for l in range(10):
            if l < 2:
                body = low_ref[c * 2 + l].astype(F32)
            elif l < 8:
                body = lam_ref[c, l - 2]
                total = total + profile_ref[c, l - 2] * body
            else:
                body = high_ref[c * 2 + l - 8].astype(F32)
            scaled[l, 0:16, :] = body
            rim(
                scaled.at[l],
                48 + c * 2 + l if l < 2 else (c * 6 + l - 2 if l < 8 else 48 + c * 2 + l),
            )
            scaled[l] = scaled[l] * decays[c * 10 + l : c * 10 + l + 1, :]
        surface_ref[c] = total

        def both(l):
            at = c * 10 + l
            return decays[at : at + 1, :] * gains[l : l + 1, :]

        for l in range(1, 9):
            here = scaled[l]
            above, below = kzs[l], kzs[l - 1]
            mixed_ref[c, l - 1] = (
                here + above * (scaled[l + 1] - here) - below * (here - scaled[l - 1])
            )
            gain = both(l)
            coef_ref[c, l - 1] = (
                gain + above * (both(l + 1) - gain) - below * (gain - both(l - 1))
            )


def roll(x, shift, axis):
    return pltpu.roll(x, shift % x.shape[axis], axis)


def advect(m, cx, cy, rows):
    gx = roll(m, -1, 0) - m
    back = roll(jnp.minimum(cx, 0.0) * gx, 1, 0)
    value = m[:rows] + jnp.maximum(cx[:rows], 0.0) * gx[:rows] + back[:rows]
    m, cy = m[:rows], cy[:rows]
    gy = roll(m, -1, 1) - m
    return value + jnp.maximum(cy, 0.0) * gy + roll(jnp.minimum(cy, 0.0) * gy, 1, 1)


def first_kernel(
    gain_ref,
    profile_ref,
    cxs,
    cys,
    mixed_ref,
    coef_ref,
    early_ref,
    decays,
    map_ref,
    later_ref,
    surface_ref,
    blocks,
    field,
):
    cols = early_ref.shape[2]
    groups, parts = cols // 128, map_ref.shape[0]
    total = map_ref[0]
    for k in range(1, parts):
        total = total + map_ref[k]
    blocks[0:144, :] = total[0:144]
    blocks[144:176, :] = jnp.zeros((32, 128), F32)
    blocks[176:192, :] = total[144:160]
    for q in range(groups):
        field[:, q * 128 : (q + 1) * 128] = blocks[pl.ds(q, ROWS, stride=groups), :]

    def tracer(c, _):
        weight = 0.0
        for l in range(6):
            weight = weight + profile_ref[c, l] * gain_ref[l]
        total = early_ref[c] + weight * field[0:16, :]
        for l in range(8):
            m = mixed_ref[c, l] + coef_ref[c, l] * field[...]
            value = advect(m, cxs[l], cys[l], ROWS)
            if 1 <= l < 7:
                total = total + profile_ref[c, l - 1] * value[0:16]
            later_ref[c, l] = decays[pl.ds(c * 10 + l + 1, 1), :] * value
        for q in range(groups):
            surface_ref[q, pl.ds(c * 16, 16), :] = total[:, q * 128 : (q + 1) * 128]
        return 0

    lax.fori_loop(0, early_ref.shape[0], tracer, 0)


def second_kernel(kzs, cxs, cys, later_ref, out_ref):
    def tracer(c, _):
        for l in range(6):
            here = later_ref[c, l + 1]
            m = (
                here
                + kzs[l + 2] * (later_ref[c, l + 2] - here)
                - kzs[l + 1] * (here - later_ref[c, l])
            )
            out_ref[c, l] = advect(m, cxs[l + 1], cys[l + 1], 16)
        return 0

    lax.fori_loop(0, out_ref.shape[0], tracer, 0)


def on_device(
    lam_in,
    courant_x,
    courant_y,
    kz_face,
    loss_rate,
    profile,
    kernel,
    obs_values,
    obs_tile,
    obs_block,
):
    size_x, size_core, size_z, size_y = SPLIT
    lev_count, tile_count = size_x * size_core, size_z * size_y
    members = lev_count * size_y
    tracers, levels, rows, cols = lam_in.shape
    blocks = rows * cols // 128
    vmem = pl.BlockSpec(memory_space=pltpu.VMEM)
    smem = pl.BlockSpec(memory_space=pltpu.SMEM)
    anywhere = pl.BlockSpec(memory_space=pl.ANY)
    shape = jax.ShapeDtypeStruct

    def call(body, outs, specs, scratch=(), flops=0, moved=0, limit=VMEM):
        return pl.pallas_call(
            body,
            out_shape=outs,
            in_specs=specs,
            out_specs=jax.tree.map(lambda _: vmem, outs),
            scratch_shapes=[pltpu.VMEM(s, F32) if isinstance(s, tuple) else s for s in scratch],
            compiler_params=pltpu.CompilerParams(vmem_limit_bytes=limit),
            cost_estimate=pl.CostEstimate(flops=flops, bytes_accessed=moved, transcendentals=0),
        )

    where = jnp.stack(
        [
            (lax.axis_index(TILE) == tile_count - 1).astype(jnp.int32),
            (lax.axis_index(LEV) == lev_count - 1).astype(jnp.int32),
        ]
    )
    decay = jnp.exp(-loss_rate)

    packed = call(
        pack_kernel,
        shape((members, 2 * CAP + 16, 128), BF16),
        [anywhere] * 3,
        scratch=[
            pltpu.VMEM((1, obs_values.shape[0]), jnp.int32),
            pltpu.VMEM((1, obs_values.shape[0]), jnp.int32),
            pltpu.VMEM(obs_values.shape, BF16),
            (obs_values.shape[0] + 2 * CAP, 128),
            pltpu.VMEM((8, 128), jnp.int32),
            pltpu.SMEM((8, 128), jnp.int32),
            pltpu.SemaphoreType.DMA((4,)),
        ],
        flops=1 << 30,
        moved=2 << 20,
        limit=MOST,
    )(obs_tile.reshape(1, -1), obs_block.reshape(1, -1), obs_values)
    got = lax.all_to_all(packed, LEV + ("y",), 0, 0, tiled=True)

    up, down, own_prior, own_next = call(
        level_kernel,
        (
            shape((14, rows, cols), BF16),
            shape((13, rows, cols), BF16),
            shape((OWN, cols), BF16),
            shape((OWN, cols), BF16),
        ),
        [smem] * 3 + [vmem] * 4 + [anywhere],
        scratch=[(OWN, cols)],
        moved=4 << 20,
        limit=MOST,
    )(where, decay, kernel, lam_in, kz_face, courant_x, courant_y, packed)
    low = chain(LEV, lev_count, 1)(up)
    high = chain(LEV, lev_count, -1)(down)
    first_rows, last_rows = call(
        row_kernel,
        (shape((STRIP, cols), BF16), shape((STRIP, cols), BF16)),
        [vmem] * 4,
        scratch=[(STRIP - OWN, cols)],
        moved=2 << 20,
    )(own_prior, own_next, low, high)
    after = chain(TILE, tile_count, -1)(first_rows)
    prior = chain(TILE, tile_count, 1)(last_rows)
    kzs, cxs, cys, mixed, coef, early, decays = call(
        ready_kernel,
        (
            shape((9, ROWS, cols), F32),
            shape((8, ROWS, cols), F32),
            shape((8, ROWS, cols), F32),
            shape((tracers, 8, ROWS, cols), F32),
            shape((tracers, 8, ROWS, cols), F32),
            shape((tracers, rows, cols), F32),
            shape((10 * tracers, cols), F32),
        ),
        [smem] * 4 + [vmem] * 8,
        scratch=[(STRIP, cols), (STRIP, cols), (16, cols), (10, ROWS, cols)],
        moved=12 << 20,
    )(
        where,
        decay,
        kernel,
        profile,
        lam_in,
        kz_face,
        courant_x,
        courant_y,
        low,
        high,
        after,
        prior,
    )

    sums = call(
        sum_kernel, shape((2, blocks, 128), F32), [vmem], flops=1 << 28, moved=1 << 20
    )(got)

    def along_z(value, j):
        perm = [
            (k * size_z + z, k * size_z + (z + SHIFTS[k][j]) % size_z)
            for k in range(lev_count)
            for z in range(size_z)
        ]
        return lax.ppermute(value, LEV + ("z",), perm)

    part = along_z(sums[0], 0) + along_z(sums[1], 1)
    edge = 2 * cols // 128
    part_after = chain(TILE, tile_count, -1)(part[:edge])
    part_prior = chain(TILE, tile_count, 1)(part[-edge:])
    parts = lax.all_gather(jnp.concatenate([part, part_after, part_prior]), LEV, axis=0)

    later, surface = call(
        first_kernel,
        (
            shape((tracers, 8, ROWS, cols), F32),
            shape((lev_count, tracers * rows, cols // lev_count), F32),
        ),
        [smem] * 2 + [vmem] * 7,
        scratch=[(ROWS * cols // 128, 128), (ROWS, cols)],
        moved=8 << 20,
    )(kernel, profile, cxs, cys, mixed, coef, early, decays, parts)
    shares = lax.all_to_all(surface, LEV, 0, 0, tiled=True)
    lam_out = call(
        second_kernel, shape(lam_in.shape, F32), [vmem] * 4, moved=6 << 20
    )(kzs, cxs, cys, later)
    gradient = jnp.sum(shares, axis=0).reshape(tracers, rows, cols // lev_count)
    return lam_out, gradient


def solution(mesh):
    grid = Mesh(np.asarray(mesh.devices).reshape(SPLIT), ("x", "core", "z", "y"))
    in_specs = (
        P(None, LEV, TILE, None),
        P(LEV, TILE, None),
        P(LEV, TILE, None),
        P(LEV, TILE, None),
        P(None, LEV),
        P(None, LEV),
        P(LEV),
        P(LEV + TILE, None),
        P(LEV + TILE, None),
        P(LEV + TILE),
    )
    out_specs = (P(None, LEV, TILE, None), P(None, TILE, LEV))
    return jax.shard_map(
        on_device, mesh=grid, in_specs=in_specs, out_specs=out_specs, check_vma=False
    )
```
